32 devices in a mesh: sib: 2 (over core), row: 4 (over z), col: 4 (over y, x).
Axes of the slice: x: 2, y: 2, z: 4, core: 2. Of those that a mesh axis runs over, the one named last changes fastest.
Arguments:
- front_inverse: bfloat16 [24576, 24576], P('row', 'col'), may hold values from -0.078125 to 0.078125
- panel: bfloat16 [2, 12288, 256], P('sib', 'col'), may hold values from -0.59765625 to 0.59765625
- row_map: int32 [2, 12288], P('sib'), may hold values from 0 to 24575, as said below
- diag_inverse: float32 [2, 256, 256], P('sib'), may hold values from -6 to 6
Outputs:
- offdiag_block: float32 [2, 24576, 256], P('sib', ('row', 'col'))
- diag_block: float32 [2, 256, 256], P('sib')
The draws below stay inside these ranges and needn't reach their ends.
Inputs may be any that keep to these rules, and one draw needn't show every extreme that they name: Each row of row_map names 12288 different front rows in increasing order, the first 0 and the last 24575.
All inputs are finite; a program needn't handle non-finite values.
Results may differ from the reference program's by a relative error of at most 0.0003.
Values may be sent and summed in bfloat16 or wider, within the bound.
No kernel may reach another device: no remote copies, remote signals or barrier semaphores. Data moves between devices by JAX's collectives and lax.ppermute only.
A program may use at most 128 MiB of HBM per device.

```python
import jax
import jax.numpy as jnp
from jax import lax

F = 24576
W = 256
R = 12288


def chosen_rows(key, which):
    base = jax.random.fold_in(key, 71 + which)
    block = F // 16
    levels = jnp.array([4, 4, 4, 4, 4, 2, 2, 2, 2, 1, 1, 1, 1, 0, 0, 0], jnp.int32)
    counts = jax.random.permutation(jax.random.fold_in(base, 5), levels) * (block // 4)
    block_keys = jax.random.split(jax.random.fold_in(base, 9), 16)
    ranks = jax.vmap(lambda k: jax.random.permutation(k, block))(block_keys)
    picked = (ranks < counts[:, None]).reshape(F)
    index = jnp.arange(F, dtype=jnp.int32)
    order_keys = jnp.where(picked, index, index + F).astype(jnp.int32)
    ordered = jnp.argsort(order_keys, stable=True).astype(jnp.int32)
    rows = ordered[:R]
    rows = rows.at[0].set(0)
    rows = rows.at[R - 1].set(F - 1)
    return rows.astype(jnp.int32)


def draw_row_map(key, part):
    return jnp.stack([chosen_rows(key, 0), chosen_rows(key, 1)]).astype(jnp.int32)


def spiked(drawn, stream_key, source, target, blocks, factor):
    def block_of(axis_at):
        return (jnp.arange(drawn.shape[axis_at]) // (drawn.shape[axis_at] // blocks)).reshape((-1,) + (1,) * (drawn.ndim - 1 - axis_at))

    first = jax.random.permutation(stream_key, blocks)[block_of(target)]
    second = (block_of(target) + blocks // 2) % blocks
    return jnp.where((block_of(source) == first) | (block_of(source) == second), factor * drawn, drawn)


def steps_of(rng, dims, shards, least, largest):
    factor_of, own = 1.0, jax.random.fold_in(rng, 6)
    for dim, blocks in shards:
        heights = jnp.exp(jax.random.uniform(jax.random.fold_in(own, dim), (blocks,), jnp.float32, least / len(shards), largest / len(shards)))
        factor_of = factor_of * jnp.repeat(heights, dims[dim] // blocks).reshape([-1 if axis == dim else 1 for axis in range(len(dims))])
    return factor_of


def scatter_about(stream_key, shape, scale, bound, cuts=(), kind=jnp.bfloat16):
    loudness = steps_of(stream_key, shape, cuts, -0.22, 0.18) if cuts else 1.0
    entries = jax.random.normal(stream_key, shape, jnp.float32) * scale * loudness
    return jnp.minimum(jnp.maximum(entries, -bound), bound).astype(kind)


def noise_with(own_key, shape, width, most, pieces, heavy, kind=jnp.bfloat16):
    values = width * jax.random.normal(own_key, shape, jnp.float32)
    if pieces:
        values = values * steps_of(own_key, shape, pieces, -0.22, 0.18)
    return jnp.clip(spiked(values, jax.random.fold_in(own_key, 3), *heavy), -most, most).astype(kind)


def setup_inputs(seed: int = 0) -> dict:
    key_of = jax.random.split(jax.random.key(seed), 5)
    front_inverse = noise_with(key_of[0], (F, F), R ** -0.5, 0.078125, ((0, 4), (1, 4)), (1, 0, 4, 2.0))
    panel = scatter_about(key_of[1], (2, R, W), 0.1, 0.59765625, ((0, 2), (1, 4)))
    row_map = draw_row_map(jax.random.fold_in(key_of[4], 71), 0)
    diag_inverse = scatter_about(key_of[3], (2, W, W), 1.0, 6.0, ((0, 2),), jnp.float32)
    return {"front_inverse": front_inverse, "panel": panel, "row_map": row_map, "diag_inverse": diag_inverse}


def one_panel(front_inverse, rows, places, diag_part):
    spread = jnp.zeros((F, W), jnp.bfloat16).at[places].set(rows)
    product = jnp.dot(front_inverse, spread, preferred_element_type=jnp.float32)
    marks = jnp.zeros((F,), jnp.float32).at[places].set(1.0)
    offdiag = jnp.where(marks[:, None] > 0.5, -product, jnp.zeros_like(product))
    diag = diag_part + jnp.dot(spread.astype(jnp.float32).T, product, precision=lax.Precision.HIGHEST)
    return offdiag, diag


def reference(front_inverse, panel, row_map, diag_inverse):
    first_off, first_diag = one_panel(front_inverse, panel[0], row_map[0], diag_inverse[0])
    second_off, second_diag = one_panel(front_inverse, panel[1], row_map[1], diag_inverse[1])
    return (jnp.stack([first_off, second_off]), jnp.stack([first_diag, second_diag]))
```

```python
import functools
import math

import jax
import jax.numpy as jnp
from jax import lax
from jax.experimental import pallas as pl
from jax.experimental.pallas import tpu as pltpu
from jax.sharding import PartitionSpec as P

LANES = 128
TILE = 256
WINDOW = TILE + LANES
GROUP = 64
STEPS = 256.0
TOP = 32766.0
VMEM = 56 * 1024 * 1024


def window_hits(map_ref, begin, target):
    first = lax.div(begin, LANES)
    row = jnp.concatenate([map_ref[first + j] for j in range(WINDOW // LANES)], axis=1)
    wanted = lax.broadcasted_iota(jnp.int32, (TILE, WINDOW), 0) + target
    return wanted == row


def spread_tile(panel_ref, map_ref, begin, offset, target):
    table = jnp.where(window_hits(map_ref, begin, target), 1.0, 0.0).astype(jnp.bfloat16)
    local = pl.multiple_of(begin - offset, LANES)
    rows = panel_ref[pl.ds(local, WINDOW), :]
    return jnp.dot(table, rows, preferred_element_type=jnp.float32).astype(jnp.bfloat16)


def window_begin(first, low, high):
    return jnp.clip(first // LANES * LANES, low, high - WINDOW)


def multiply_into(total_ref, front_ref, tile):
    rows = total_ref.shape[0]
    chunk = math.gcd(rows, 512)

    @pl.loop(0, rows // chunk)
    def _(m):
        at = pl.ds(pl.multiple_of(m * chunk, chunk), chunk)
        total_ref[at, :] += jnp.dot(front_ref[at, :], tile, preferred_element_type=jnp.float32)


def own_kernel(tiles, meta, begins, front_ref, panel_ref, map_ref, total_ref):
    step = pl.program_id(0)

    @pl.when(step == 0)
    def _():
        total_ref[...] = jnp.zeros_like(total_ref)

    @pl.when(step < meta[0])
    def _():
        k = tiles[step]
        tile = spread_tile(panel_ref, map_ref, begins[k], meta[1], meta[2] + k * TILE)
        multiply_into(total_ref, front_ref, tile)


def own_product(front, panel, map3, tiles, meta, begins):
    rows, cols = front.shape
    width = panel.shape[1]
    return pl.pallas_call(
        own_kernel,
        grid_spec=pltpu.PrefetchScalarGridSpec(
            num_scalar_prefetch=3,
            grid=(cols // TILE,),
            in_specs=[
                pl.BlockSpec((rows, TILE), lambda i, t, m, b: (0, t[i])),
                pl.BlockSpec(panel.shape, lambda i, t, m, b: (0, 0)),
                pl.BlockSpec(map3.shape, lambda i, t, m, b: (0, 0, 0)),
            ],
            out_specs=pl.BlockSpec((rows, width), lambda i, t, m, b: (0, 0)),
        ),
        out_shape=jax.ShapeDtypeStruct((rows, width), jnp.float32),
        compiler_params=pltpu.CompilerParams(vmem_limit_bytes=VMEM),
        cost_estimate=pl.CostEstimate(
            flops=2 * rows * cols * width, bytes_accessed=2 * rows * cols, transcendentals=0
        ),
        name="own_product",
    )(tiles, meta, begins, front, panel, map3)


def quantized(values, out_ref):
    rows, width = values.shape[0], values.shape[1]
    codes = []
    for g in range(rows // GROUP):
        part = values[g * GROUP:(g + 1) * GROUP, :]
        most = jnp.max(jnp.abs(part), axis=0, keepdims=True)
        code = jnp.clip(jnp.ceil(jnp.log2(jnp.maximum(most, 1e-30)) * STEPS) + 1.0, -32000.0, 32000.0)
        inverse = TOP / jnp.exp2(code * (1.0 / STEPS))
        whole = jnp.clip(jnp.round(part * inverse), -TOP, TOP).astype(jnp.int32)
        out_ref[g * GROUP:(g + 1) * GROUP, :] = whole.astype(jnp.int16)
        codes.append(code)
    codes.append(jnp.zeros((out_ref.shape[0] - rows - len(codes), width), jnp.float32))
    tail = jnp.concatenate(codes, axis=0).astype(jnp.int32)
    out_ref[rows:, :] = tail.astype(jnp.int16)


def coded_rows(rows):
    return rows + (rows // GROUP + 15) // 16 * 16


def decoded(ref, rows):
    codes = ref[rows:, :].astype(jnp.int32).astype(jnp.float32)
    scales = jnp.exp2(codes * (1.0 / STEPS)) * (1.0 / TOP)
    parts = []
    for g in range(rows // GROUP):
        part = ref[g * GROUP:(g + 1) * GROUP, :].astype(jnp.int32).astype(jnp.float32)
        parts.append(part * scales[g:g + 1, :])
    return jnp.concatenate(parts, axis=0)


def rest_kernel(
    half, tiles, meta, begins, front_ref, map_ref, start_ref, own, along_x, along_y, low_far, high_far,
    total_out, ax1, by1, ax2, by2, panel, total, sems,
):
    step = pl.program_id(0)
    shard = own.shape[0]
    me = meta[1]
    count = meta[0]

    def assembly():
        far = pl.multiple_of((me ^ 3) * shard, LANES)
        return [
            pltpu.make_async_copy(start_ref, total, sems.at[0]),
            pltpu.make_async_copy(own, panel.at[pl.ds(pl.multiple_of(me * shard, LANES), shard)], sems.at[1]),
            pltpu.make_async_copy(along_x, panel.at[pl.ds(pl.multiple_of((me ^ 1) * shard, LANES), shard)], sems.at[2]),
            pltpu.make_async_copy(along_y, panel.at[pl.ds(pl.multiple_of((me ^ 2) * shard, LANES), shard)], sems.at[3]),
            pltpu.make_async_copy(low_far, panel.at[pl.ds(far, shard // 2)], sems.at[4]),
            pltpu.make_async_copy(high_far, panel.at[pl.ds(far + shard // 2, shard // 2)], sems.at[5]),
        ]

    @pl.when(step == 0)
    def _():
        copies = assembly()
        for copy in copies:
            copy.start()
        for copy in copies:
            copy.wait()

    @pl.when(step < count)
    def _():
        k = tiles[step]
        tile = spread_tile(panel, map_ref, begins[k], 0, meta[2] + k * TILE)
        multiply_into(total, front_ref, tile)

    @pl.when(step == pl.num_programs(0) - 1)
    def _():
        out = pltpu.make_async_copy(total, total_out, sems.at[0])
        out.start()

        def block(which, part):
            return total[pl.ds(pl.multiple_of((which * 2 + part) * half, half), half), :]

        quantized(block(me ^ 3, 0), ax1)
        quantized(block(me ^ 3, 1), by1)
        quantized(block(me ^ 1, 0), ax2)
        quantized(block(me ^ 2, 1), by2)
        out.wait()


def rest_product(front, map3, start, own, along_x, along_y, low_far, high_far, tiles, meta, begins, half):
    rows, cols = front.shape
    shard, width = own.shape
    total_rows = map3.shape[0] * LANES
    coded = coded_rows(half)
    anywhere = pl.BlockSpec(memory_space=pl.ANY)
    payload = pl.BlockSpec((coded, width), lambda i, t, m, b: (0, 0))
    return pl.pallas_call(
        functools.partial(rest_kernel, half),
        grid_spec=pltpu.PrefetchScalarGridSpec(
            num_scalar_prefetch=3,
            grid=(cols // TILE,),
            in_specs=[
                pl.BlockSpec((rows, TILE), lambda i, t, m, b: (0, t[i])),
                pl.BlockSpec(map3.shape, lambda i, t, m, b: (0, 0, 0)),
            ] + [anywhere] * 6,
            out_specs=[anywhere] + [payload] * 4,
            scratch_shapes=[
                pltpu.VMEM((total_rows, width), jnp.bfloat16),
                pltpu.VMEM((rows, width), jnp.float32),
                pltpu.SemaphoreType.DMA((6,)),
            ],
        ),
        out_shape=[jax.ShapeDtypeStruct((rows, width), jnp.float32)]
        + [jax.ShapeDtypeStruct((coded, width), jnp.int16)] * 4,
        compiler_params=pltpu.CompilerParams(vmem_limit_bytes=VMEM),
        cost_estimate=pl.CostEstimate(
            flops=rows * cols * width, bytes_accessed=rows * cols, transcendentals=0
        ),
        name="rest_product",
    )(tiles, meta, begins, front, map3, start, own, along_x, along_y, low_far, high_far)


def diag_kernel(meta, begins, total_ref, map_ref, own, along_x, along_y, low_far, high_far, diag_ref, panel, sems):
    step = pl.program_id(0)
    shard = own.shape[0]
    me = meta[0]

    @pl.when(step == 0)
    def _():
        far = pl.multiple_of((me ^ 3) * shard, LANES)
        copies = [
            pltpu.make_async_copy(own, panel.at[pl.ds(pl.multiple_of(me * shard, LANES), shard)], sems.at[0]),
            pltpu.make_async_copy(along_x, panel.at[pl.ds(pl.multiple_of((me ^ 1) * shard, LANES), shard)], sems.at[1]),
            pltpu.make_async_copy(along_y, panel.at[pl.ds(pl.multiple_of((me ^ 2) * shard, LANES), shard)], sems.at[2]),
            pltpu.make_async_copy(low_far, panel.at[pl.ds(far, shard // 2)], sems.at[3]),
            pltpu.make_async_copy(high_far, panel.at[pl.ds(far + shard // 2, shard // 2)], sems.at[4]),
        ]
        for copy in copies:
            copy.start()
        diag_ref[...] = jnp.zeros_like(diag_ref)
        for copy in copies:
            copy.wait()

    tile = spread_tile(panel, map_ref, begins[step], 0, meta[1] + step * TILE)
    values = total_ref[...]
    high = values.astype(jnp.bfloat16)
    low = (values - high.astype(jnp.float32)).astype(jnp.bfloat16)
    across = (((0,), (0,)), ((), ()))
    diag_ref[...] += lax.dot_general(tile, high, across, preferred_element_type=jnp.float32)
    diag_ref[...] += lax.dot_general(tile, low, across, preferred_element_type=jnp.float32)


def diag_product(total, map3, own, along_x, along_y, low_far, high_far, meta, begins):
    rows, width = total.shape
    anywhere = pl.BlockSpec(memory_space=pl.ANY)
    return pl.pallas_call(
        diag_kernel,
        grid_spec=pltpu.PrefetchScalarGridSpec(
            num_scalar_prefetch=2,
            grid=(rows // TILE,),
            in_specs=[
                pl.BlockSpec((TILE, width), lambda i, m, b: (i, 0)),
                pl.BlockSpec(map3.shape, lambda i, m, b: (0, 0, 0)),
            ] + [anywhere] * 5,
            out_specs=pl.BlockSpec((width, width), lambda i, m, b: (0, 0)),
            scratch_shapes=[
                pltpu.VMEM((map3.shape[0] * LANES, width), jnp.bfloat16),
                pltpu.SemaphoreType.DMA((5,)),
            ],
        ),
        out_shape=jax.ShapeDtypeStruct((width, width), jnp.float32),
        compiler_params=pltpu.CompilerParams(vmem_limit_bytes=VMEM),
        cost_estimate=pl.CostEstimate(
            flops=6 * rows * width * width, bytes_accessed=8 * rows * width, transcendentals=0
        ),
        name="diag_product",
    )(meta, begins, total, map3, own, along_x, along_y, low_far, high_far)


def second_kernel(where, low_ref, high_ref, low_in, high_in, low_out, high_out):
    rows = low_ref.shape[0]
    quantized(low_ref[...] + decoded(low_in, rows), low_out)
    quantized(high_ref[...] + decoded(high_in, rows), high_out)


def second_hop(total, low_in, high_in, where, half):
    width = total.shape[1]
    coded = low_in.shape[0]
    payload = pl.BlockSpec((coded, width), lambda i, w: (0, 0))
    return pl.pallas_call(
        second_kernel,
        grid_spec=pltpu.PrefetchScalarGridSpec(
            num_scalar_prefetch=1,
            grid=(1,),
            in_specs=[
                pl.BlockSpec((half, width), lambda i, w: (w[0], 0)),
                pl.BlockSpec((half, width), lambda i, w: (w[1], 0)),
                payload,
                payload,
            ],
            out_specs=[payload, payload],
        ),
        out_shape=[jax.ShapeDtypeStruct((coded, width), jnp.int16)] * 2,
        compiler_params=pltpu.CompilerParams(vmem_limit_bytes=VMEM),
        cost_estimate=pl.CostEstimate(
            flops=8 * half * width, bytes_accessed=16 * half * width, transcendentals=0
        ),
        name="second_hop",
    )(where, total, total, low_in, high_in)


def last_kernel(where, begins, low_ref, high_ref, low_1, low_2, high_1, high_2, map_ref, out_ref):
    rows = low_ref.shape[0]
    sums = [
        low_ref[...] + decoded(low_1, rows) + decoded(low_2, rows),
        high_ref[...] + decoded(high_1, rows) + decoded(high_2, rows),
    ]
    for part, value in enumerate(sums):
        for j in range(rows // TILE):
            n = part * (rows // TILE) + j
            hits = window_hits(map_ref, begins[n], where[2] + n * TILE)
            marked = jnp.max(jnp.where(hits, 1.0, 0.0), axis=1, keepdims=True)
            tile = value[j * TILE:(j + 1) * TILE, :]
            out_ref[n * TILE:(n + 1) * TILE, :] = jnp.where(marked > 0.5, -tile, 0.0)


def last_sum(total, low_1, low_2, high_1, high_2, map3, where, begins, half):
    width = total.shape[1]
    payload = pl.BlockSpec(low_1.shape, lambda i, w, b: (0, 0))
    return pl.pallas_call(
        last_kernel,
        grid_spec=pltpu.PrefetchScalarGridSpec(
            num_scalar_prefetch=2,
            grid=(1,),
            in_specs=[
                pl.BlockSpec((half, width), lambda i, w, b: (w[0], 0)),
                pl.BlockSpec((half, width), lambda i, w, b: (w[1], 0)),
                payload,
                payload,
                payload,
                payload,
                pl.BlockSpec(map3.shape, lambda i, w, b: (0, 0, 0)),
            ],
            out_specs=pl.BlockSpec((2 * half, width), lambda i, w, b: (0, 0)),
        ),
        out_shape=jax.ShapeDtypeStruct((2 * half, width), jnp.float32),
        compiler_params=pltpu.CompilerParams(vmem_limit_bytes=VMEM),
        cost_estimate=pl.CostEstimate(
            flops=16 * half * width, bytes_accessed=24 * half * width, transcendentals=0
        ),
        name="last_sum",
    )(where, begins, total, total, low_1, low_2, high_1, high_2, map3)


def listed(chosen):
    n = chosen.shape[0]
    index = jnp.arange(n, dtype=jnp.int32)
    before = jnp.sum((index[None, :] <= index[:, None]) & chosen[None, :], axis=1, dtype=jnp.int32)
    count = jnp.sum(chosen, dtype=jnp.int32)
    place = jnp.minimum(index, jnp.maximum(count - 1, 0))
    hit = (before[None, :] - 1 == place[:, None]) & chosen[None, :]
    return jnp.sum(jnp.where(hit, index[None, :], 0), axis=1, dtype=jnp.int32), count


def reduced(block, axis):
    n = lax.axis_size(axis)
    me = lax.axis_index(axis)
    share = block.shape[0] // n

    def shifted(value, by):
        return lax.ppermute(value, axis, [(i, (i + by) % n) for i in range(n)])

    def part(of):
        return lax.dynamic_slice_in_dim(block, lax.rem(of, n) * share, share, 0)

    arrived = [shifted(part(me + by), by) for by in range(1, n)]
    return sum(arrived, part(me)), shifted


def spread_out(mine, shifted, axis):
    n = lax.axis_size(axis)
    me = lax.axis_index(axis)
    share = mine.shape[0]
    whole = jnp.zeros((n * share,) + mine.shape[1:], mine.dtype)
    for by in range(n):
        value = mine if by == 0 else shifted(mine, by)
        whole = lax.dynamic_update_slice_in_dim(whole, value, lax.rem(me - by + n, n) * share, 0)
    return whole


def four_columns(front, panel, row_map, diag_inverse):
    me = lax.axis_index("col")
    rows, cols = front.shape
    own = panel[0]
    shard, width = own.shape
    share = rows // 4
    half = share // 2
    places = row_map[0]
    map3 = places.reshape(-1, 1, LANES)
    total_rows = places.shape[0]

    def partner(value, bit):
        return lax.ppermute(value, "col", [(i, i ^ bit) for i in range(4)])

    along_x = partner(own, 1)
    along_y = partner(own, 2)
    low_far = partner(along_x[: shard // 2], 2)
    high_far = partner(along_y[shard // 2:], 1)

    col_base = me * cols
    row_base = lax.axis_index("row") * rows
    col_marks = col_base + TILE * jnp.arange(cols // TILE + 1, dtype=jnp.int32)
    row_marks = row_base + TILE * jnp.arange(rows // TILE, dtype=jnp.int32)
    marks = jnp.concatenate([col_marks, row_marks])
    before = jnp.sum(places[None, :] < marks[:, None], axis=1, dtype=jnp.int32)
    col_first = before[: cols // TILE + 1]
    row_first = before[cols // TILE + 1:]
    low, high = me * shard, (me + 1) * shard
    some = col_first[1:] > col_first[:-1]
    inside = (col_first[:-1] >= low) & (col_first[1:] <= high)
    own_tiles, own_count = listed(some & inside)
    rest_tiles, rest_count = listed(some & ~inside)
    own_begins = window_begin(col_first, low, high)
    col_begins = window_begin(col_first, 0, total_rows)
    row_begins = window_begin(row_first, 0, total_rows)

    start = own_product(front, own, map3, own_tiles, jnp.stack([own_count, low, col_base]), own_begins)
    total, ax1, by1, ax2, by2 = rest_product(
        front, map3, start, own, along_x, along_y, low_far, high_far,
        rest_tiles, jnp.stack([rest_count, me, col_base]), col_begins, half,
    )
    ax1 = partner(ax1, 1)
    by1 = partner(by1, 2)
    ax2 = partner(ax2, 1)
    by2 = partner(by2, 2)
    terms = diag_product(
        total, map3, own, along_x, along_y, low_far, high_far, jnp.stack([me, row_base]), row_begins
    )
    low_2, high_2 = second_hop(
        total, ax1, by1, jnp.stack([(me ^ 2) * 2, (me ^ 1) * 2 + 1]), half
    )
    low_2 = partner(low_2, 2)
    high_2 = partner(high_2, 1)

    mine, shifted = reduced(terms, "row")
    mine = mine + partner(mine, 1)
    mine = mine + partner(mine, 2)
    diag = diag_inverse[0] + spread_out(mine, shifted, "row")

    tiles = share // TILE
    offdiag = last_sum(
        total, ax2, low_2, by2, high_2, map3,
        jnp.stack([me * 2, me * 2 + 1, row_base + me * share]),
        lax.dynamic_slice_in_dim(row_begins, me * tiles, tiles, 0), half,
    )
    return offdiag[None], diag[None]


def spread_range(padded_rows, padded_places, places, lower, count):
    blk = math.gcd(count, 128)
    nblk = count // blk
    starts = lower + jnp.arange(nblk, dtype=jnp.int32) * blk
    first = jnp.searchsorted(places, starts)

    def window(begin):
        rows = lax.dynamic_slice_in_dim(padded_rows, begin, blk, 0)
        marks = lax.dynamic_slice_in_dim(padded_places, begin, blk, 0)
        return (rows, marks)

    rows, marks = jax.vmap(window)(first)
    target = starts[:, None] + jnp.arange(blk, dtype=jnp.int32)[None, :]
    onehot = marks[:, None, :] == target[:, :, None]
    table = onehot.astype(jnp.bfloat16)
    spread = jnp.einsum("njk,nkw->njw", table, rows, preferred_element_type=jnp.float32)
    hits = jnp.sum(onehot.astype(jnp.float32), axis=2)
    return (spread.astype(jnp.bfloat16).reshape(count, rows.shape[2]), hits.reshape(count))


def any_columns(front_inverse, panel, row_map, diag_inverse):
    row_index = lax.axis_index("row")
    col_index = lax.axis_index("col")
    ncol = lax.axis_size("col")
    front_rows, front_cols = front_inverse.shape
    share = front_rows // ncol
    width = panel.shape[2]
    col_lower = col_index * front_cols
    row_lower = row_index * front_rows
    share_lower = row_lower + col_index * share
    places_all = row_map[0]
    whole_panel = lax.all_gather(panel, "col", axis=1, tiled=True)[0]
    padded_rows = jnp.concatenate([whole_panel, jnp.zeros((128, width), jnp.bfloat16)], axis=0)
    total_front = front_rows * lax.axis_size("row")
    padded_places = jnp.concatenate([places_all, jnp.full((128,), total_front, jnp.int32)], axis=0)
    spread_cols, unused_hits = spread_range(
        padded_rows, padded_places, places_all, col_lower, front_cols
    )
    spread_rows, share_hits = spread_range(
        padded_rows, padded_places, places_all, share_lower, share
    )
    product = lax.psum_scatter(
        jnp.dot(front_inverse, spread_cols, preferred_element_type=jnp.float32),
        "col",
        scatter_dimension=0,
        tiled=True,
    )
    local_terms = jnp.dot(
        spread_rows.astype(jnp.float32).T, product, precision=lax.Precision.HIGHEST
    )
    diag_terms = lax.psum(local_terms, ("row", "col"))
    offdiag = jnp.where(share_hits[:, None] > 0.5, -product, jnp.zeros_like(product))
    diag = diag_inverse[0] + diag_terms
    return (offdiag[None], diag[None])


def solution(mesh):
    return jax.shard_map(
        four_columns if mesh.shape["col"] == 4 else any_columns,
        mesh=mesh,
        in_specs=(P("row", "col"), P("sib", "col", None), P("sib", None), P("sib", None, None)),
        out_specs=(P("sib", ("row", "col"), None), P("sib", None, None)),
        check_vma=False,
    )
```

```python
import functools

import jax
import jax.numpy as jnp
from jax import lax
from jax.experimental import pallas as pl
from jax.experimental.pallas import tpu as pltpu
from jax.sharding import PartitionSpec as P
import math

LANES = 128
TILE = 256
WINDOW = TILE + LANES
STRIP = 2 * TILE
SLOTS = 3
GROUP = 64
STEPS = 256.0
TOP = 32766.0
LIMIT = 40 * 1024 * 1024
FIRST = 3
KERNELS = 3
GROUP_TILES = 4
SMALL = pl.CostEstimate(flops=1000, bytes_accessed=1000, transcendentals=0)
LAST = 2


class Layout:
    def __init__(self, rows, cols):
        self.strips = cols // STRIP
        self.col_tiles = cols // TILE
        self.row_tiles = rows // TILE
        self.counts = 0
        self.lists = KERNELS
        self.col_begins = self.lists + KERNELS * self.strips
        self.row_begins = self.col_begins + self.col_tiles
        self.row_phases = self.row_begins + self.row_tiles
        self.me = self.row_phases + self.row_tiles
        self.col_base = self.me + 1
        self.row_base = self.me + 2
        self.size = self.me + 3


def near_half(shard):
    return 1 - lax.rem(shard, 2)


def arrival(block, me):
    shard = lax.div(block, 2)
    near = lax.rem(block, 2) == near_half(shard)
    away = shard ^ me
    first = (away != 3) & (near == (away == 1))
    return jnp.where(away == 0, 0, jnp.where(first, 1, 2))


def plan_kernel(at, half, total_rows, before, place, own, plan, near, far, kept, sems):
    me = place[0]
    arriving = pltpu.make_async_copy(own, kept, sems.at[0])
    arriving.start()
    copies = []
    for n, (which, out) in enumerate(((near_half(me), near), (1 - near_half(me), far))):
        source = kept.at[pl.ds(pl.multiple_of(which * half, LANES), half)]
        copies.append(pltpu.make_async_copy(source, out, sems.at[n + 1]))

    def phase(first, last):
        start = arrival(lax.div(first, half), me)
        end = arrival(lax.div(last - 1, half), me)
        return jnp.maximum(start, end)

    def begin(first):
        return jnp.minimum(lax.div(first, LANES) * LANES, total_rows - WINDOW)

    for i in range(KERNELS * at.strips):
        plan[at.lists + i] = 0
    counts = [jnp.int32(0)] * KERNELS
    per = STRIP // TILE
    for s in range(at.strips):
        first, last = before[s * per], before[(s + 1) * per]
        when = phase(first, last)
        some = last > first
        taken = jnp.bool_(False)
        for j in range(KERNELS):
            fits = some & (when <= j) & ~taken
            if j == 0:
                fits = fits & (counts[j] < FIRST)

            @pl.when(fits)
            def _():
                plan[at.lists + j * at.strips + counts[j]] = s

            counts[j] = counts[j] + jnp.where(fits, 1, 0)
            taken = taken | fits
    arriving.wait()
    for copy in copies:
        copy.start()
    for j in range(KERNELS):
        plan[at.counts + j] = counts[j]
    for k in range(at.col_tiles):
        plan[at.col_begins + k] = begin(before[k])
    base = at.col_tiles + 1
    for k in range(at.row_tiles):
        first, last = before[base + k], before[base + k + 1]
        plan[at.row_begins + k] = begin(first)
        plan[at.row_phases + k] = jnp.where(last > first, phase(first, last), 0)
    for i in range(3):
        plan[at.me + i] = place[i]
    for copy in copies:
        copy.wait()


def make_plan(at, half, total_rows, before, place, own):
    smem = pl.BlockSpec(memory_space=pltpu.SMEM)
    hbm = pl.BlockSpec(memory_space=pltpu.HBM)
    piece = jax.ShapeDtypeStruct((half, own.shape[1]), own.dtype)
    return pl.pallas_call(
        functools.partial(plan_kernel, at, half, total_rows),
        in_specs=[smem, smem, hbm],
        out_specs=[smem, hbm, hbm],
        out_shape=[jax.ShapeDtypeStruct((at.size,), jnp.int32), piece, piece],
        scratch_shapes=[pltpu.VMEM(own.shape, own.dtype), pltpu.SemaphoreType.DMA((3,))],
        compiler_params=pltpu.CompilerParams(vmem_limit_bytes=LIMIT),
        cost_estimate=SMALL,
        name="plan",
    )(before, place, own)


def window_hits(map_ref, begin, target):
    first = lax.div(begin, LANES)
    row = jnp.concatenate([map_ref[first + j] for j in range(WINDOW // LANES)], axis=1)
    wanted = lax.broadcasted_iota(jnp.int32, (TILE, WINDOW), 0) + target
    return wanted == row


def spread_tile(panel_ref, map_ref, begin, target):
    table = jnp.where(window_hits(map_ref, begin, target), 1.0, 0.0).astype(jnp.bfloat16)
    rows = panel_ref[pl.ds(pl.multiple_of(begin, LANES), WINDOW), :]
    return jnp.dot(table, rows, preferred_element_type=jnp.float32).astype(jnp.bfloat16)


def strip_tile(at, s, plan, map_ref, panel, strip):
    per = STRIP // TILE
    for t in range(per):
        k = s * per + t
        strip[t * TILE:(t + 1) * TILE, :] = spread_tile(
            panel, map_ref, plan[at.col_begins + k], plan[at.col_base] + k * TILE
        )


def half_block(shard, near):
    return shard * 2 + (near_half(shard) if near else 1 - near_half(shard))


def piece_blocks(me):
    return [
        me,
        half_block(me ^ 1, True), half_block(me ^ 2, False),
        half_block(me ^ 1, False), half_block(me ^ 2, True),
        half_block(me ^ 3, True), half_block(me ^ 3, False),
    ]


def load_panel(step, me, pieces, panel, sems):
    copies = []
    for n, (piece, block) in enumerate(zip(pieces, piece_blocks(me))):
        size = piece.shape[0]
        copies.append(
            pltpu.make_async_copy(piece, panel.at[pl.ds(pl.multiple_of(block * size, LANES), size)], sems.at[n])
        )
    for copy in copies:
        copy.start()
    half = pieces[0].shape[0] // 2
    if step < LAST:
        for block in range(panel.shape[0] // half):
            @pl.when(arrival(jnp.int32(block), me) > step)
            def _():
                panel[block * half:(block + 1) * half, :] = jnp.zeros((half, panel.shape[1]), panel.dtype)
    for copy in copies:
        copy.wait()


def build_rows(at, plan, map_ref, panel, spread, group):
    size = GROUP_TILES
    for t in range(size):
        k = group * size + t
        spread[t * TILE:(t + 1) * TILE, :] = spread_tile(
            panel, map_ref, plan[at.row_begins + k], plan[at.row_base] + k * TILE
        )


def fetched(at, j, plan, front, fronts, sems, i):
    s = plan[at.lists + j * at.strips + i]
    slot = lax.rem(i, SLOTS)
    return pltpu.make_async_copy(
        front.at[:, pl.ds(pl.multiple_of(s * STRIP, STRIP), STRIP)], fronts.at[slot], sems.at[slot]
    )


def strips_begin(at, j, plan, front, fronts, sems):
    for i in range(SLOTS - 1):
        @pl.when(i < plan[at.counts + j])
        def _():
            fetched(at, j, plan, front, fronts, sems, jnp.int32(i)).start()


def strips_loop(at, j, plan, front, fronts, sems, map_ref, panel, strips, total):
    count = plan[at.counts + j]
    listed = at.lists + j * at.strips

    @pl.when(count > 0)
    def _():
        strip_tile(at, plan[listed], plan, map_ref, panel, strips.at[0])

    @pl.loop(0, count)
    def _(i):
        @pl.when(i + SLOTS - 1 < count)
        def _():
            fetched(at, j, plan, front, fronts, sems, i + SLOTS - 1).start()

        now = lax.rem(i, 2)
        following = plan[listed + jnp.minimum(i + 1, count - 1)]
        fetched(at, j, plan, front, fronts, sems, i).wait()
        total[...] += jnp.dot(fronts[lax.rem(i, SLOTS)], strips[now], preferred_element_type=jnp.float32)
        strip_tile(at, following, plan, map_ref, panel, strips.at[1 - now])


def first_kernel(at, plan, front, map_ref, own, out, total, fronts, panel, strips, sems, own_sems):
    strips_begin(at, 0, plan, front, fronts, sems)
    load_panel(0, plan[at.me], [own], panel, own_sems)
    total[...] = jnp.zeros_like(total)
    strips_loop(at, 0, plan, front, fronts, sems, map_ref, panel, strips, total)
    copy = pltpu.make_async_copy(total, out, own_sems.at[0])
    copy.start()
    copy.wait()


def next_kernel(at, n_pieces, *refs):
    plan, front, map_ref = refs[:3]
    pieces = refs[3:3 + n_pieces]
    start, total, spread, group_rows, fronts, panel, strips, sems, own_sems = refs[3 + n_pieces:]
    copy = pltpu.make_async_copy(start, total, own_sems.at[n_pieces])
    copy.start()
    strips_begin(at, 1, plan, front, fronts, sems)
    load_panel(1, plan[at.me], pieces, panel, own_sems)
    copy.wait()
    strips_loop(at, 1, plan, front, fronts, sems, map_ref, panel, strips, total)
    size = GROUP_TILES * TILE

    def written(group):
        slot = lax.rem(group, 2)
        return pltpu.make_async_copy(
            group_rows.at[slot], spread.at[pl.ds(pl.multiple_of(group * size, size), size)], own_sems.at[slot]
        )

    groups = at.row_tiles // GROUP_TILES

    @pl.loop(0, groups)
    def _(group):
        @pl.when(group >= 2)
        def _():
            written(group - 2).wait()

        build_rows(at, plan, map_ref, panel, group_rows.at[lax.rem(group, 2)], group)
        written(group).start()

    for group in range(max(groups - 2, 0), groups):
        written(jnp.int32(group)).wait()


def strips_call(kernel, at, plan, front, map3, others, out_specs, out_shape, scratch, expected, name):
    rows = front.shape[0]
    width = others[0].shape[1]
    vmem = pl.BlockSpec(memory_space=pltpu.VMEM)
    smem = pl.BlockSpec(memory_space=pltpu.SMEM)
    hbm = pl.BlockSpec(memory_space=pltpu.HBM)
    return pl.pallas_call(
        functools.partial(kernel, at),
        in_specs=[smem, hbm, vmem] + [hbm] * len(others),
        out_specs=out_specs,
        scratch_shapes=scratch + [
            pltpu.VMEM((SLOTS, rows, STRIP), jnp.bfloat16),
            pltpu.VMEM((map3.shape[0] * LANES, width), jnp.bfloat16),
            pltpu.VMEM((2, STRIP, width), jnp.bfloat16),
            pltpu.SemaphoreType.DMA((SLOTS,)),
            pltpu.SemaphoreType.DMA((max(len(others), 2),)),
        ],
        out_shape=out_shape,
        compiler_params=pltpu.CompilerParams(vmem_limit_bytes=LIMIT),
        cost_estimate=pl.CostEstimate(
            flops=8 * rows * STRIP * width * expected, bytes_accessed=8 * rows * STRIP * expected, transcendentals=0
        ),
        name=name,
    )(plan, front, map3, *others)


def first_strips(at, plan, front, map3, own):
    shape = front.shape[0], own.shape[1]
    return strips_call(
        first_kernel, at, plan, front, map3, [own], pl.BlockSpec(memory_space=pltpu.HBM), pltpu.HBM(shape, jnp.float32),
        [pltpu.VMEM(shape, jnp.float32)], FIRST, "first_strips",
    )


def next_strips(at, plan, front, map3, pieces, start):
    rows, width = start.shape
    return strips_call(
        lambda at, *refs: next_kernel(at, len(pieces), *refs), at, plan, front, map3, pieces + [start],
        [pl.BlockSpec(memory_space=pltpu.VMEM), pl.BlockSpec(memory_space=pltpu.HBM)],
        [pltpu.VMEM(start.shape, start.dtype), pltpu.HBM((rows, width), jnp.bfloat16)],
        [pltpu.VMEM((2, GROUP_TILES * TILE, width), jnp.bfloat16)], at.strips, "next_strips",
    )


def quantized(values, out_ref):
    rows, width = values.shape[0], values.shape[1]
    codes = []
    for g in range(rows // GROUP):
        part = values[g * GROUP:(g + 1) * GROUP, :]
        most = jnp.max(jnp.abs(part), axis=0, keepdims=True)
        code = jnp.clip(jnp.ceil(jnp.log2(jnp.maximum(most, 1e-30)) * STEPS) + 1.0, -32000.0, 32000.0)
        inverse = TOP / jnp.exp2(code * (1.0 / STEPS))
        whole = jnp.clip(jnp.round(part * inverse), -TOP, TOP).astype(jnp.int32)
        out_ref[g * GROUP:(g + 1) * GROUP, :] = whole.astype(jnp.int16)
        codes.append(code)
    codes.append(jnp.zeros((out_ref.shape[0] - rows - len(codes), width), jnp.float32))
    tail = jnp.concatenate(codes, axis=0).astype(jnp.int32)
    out_ref[rows:, :] = tail.astype(jnp.int16)


def coded_rows(rows):
    return rows + (rows // GROUP + 15) // 16 * 16


def decoded(ref, rows):
    codes = ref[rows:, :].astype(jnp.int32).astype(jnp.float32)
    scales = jnp.exp2(codes * (1.0 / STEPS)) * (1.0 / TOP)
    parts = []
    for g in range(rows // GROUP):
        part = ref[g * GROUP:(g + 1) * GROUP, :].astype(jnp.int32).astype(jnp.float32)
        parts.append(part * scales[g:g + 1, :])
    return jnp.concatenate(parts, axis=0)


def part_of(total, which, part):
    half = total.shape[0] // 8
    return total[pl.ds(pl.multiple_of((which * 2 + part) * half, half), half), :]


def last_strips_kernel(at, n_pieces, *refs):
    plan, front, map_ref = refs[:3]
    pieces = refs[3:3 + n_pieces]
    total, x_out, y_out, written, fronts, panel, strips, sems, own_sems = refs[4 + n_pieces:]
    me = plan[at.me]
    j = KERNELS - 1

    @pl.when(plan[at.counts + j] > 0)
    def _():
        strips_begin(at, j, plan, front, fronts, sems)
        load_panel(LAST, me, pieces, panel, own_sems)
        strips_loop(at, j, plan, front, fronts, sems, map_ref, panel, strips, total)

    coded = x_out.shape[0] // 2
    copy = pltpu.make_async_copy(total, written, own_sems.at[0])
    copy.start()
    quantized(part_of(total, me ^ 3, 0), x_out.at[:coded])
    quantized(part_of(total, me ^ 1, 0), x_out.at[coded:])
    quantized(part_of(total, me ^ 3, 1), y_out.at[:coded])
    quantized(part_of(total, me ^ 2, 1), y_out.at[coded:])
    copy.wait()


def last_strips(at, plan, front, map3, pieces, total):
    rows, width = total.shape
    coded = coded_rows(rows // 8)
    vmem = pl.BlockSpec(memory_space=pltpu.VMEM)
    smem = pl.BlockSpec(memory_space=pltpu.SMEM)
    hbm = pl.BlockSpec(memory_space=pltpu.HBM)
    return pl.pallas_call(
        functools.partial(last_strips_kernel, at, len(pieces)),
        in_specs=[smem, hbm, vmem] + [hbm] * len(pieces) + [vmem],
        out_specs=[vmem, vmem, vmem, hbm],
        scratch_shapes=[
            pltpu.VMEM((SLOTS, rows, STRIP), jnp.bfloat16),
            pltpu.VMEM((map3.shape[0] * LANES, width), jnp.bfloat16),
            pltpu.VMEM((2, STRIP, width), jnp.bfloat16),
            pltpu.SemaphoreType.DMA((SLOTS,)),
            pltpu.SemaphoreType.DMA((len(pieces),)),
        ],
        out_shape=[
            pltpu.VMEM(total.shape, total.dtype),
            jax.ShapeDtypeStruct((2 * coded, width), jnp.int16),
            jax.ShapeDtypeStruct((2 * coded, width), jnp.int16),
            pltpu.HBM(total.shape, total.dtype),
        ],
        input_output_aliases={3 + len(pieces): 0},
        compiler_params=pltpu.CompilerParams(vmem_limit_bytes=LIMIT),
        cost_estimate=SMALL,
        name="last_strips",
    )(plan, front, map3, *pieces, total)[1:]


def diag_kernel(at, n_pieces, *refs):
    plan, total_ref, early, map_ref = refs[:4]
    pieces = refs[4:4 + n_pieces]
    out, left, panel, sems = refs[4 + n_pieces:]
    step = pl.program_id(0)

    def latest(first, n):
        late = plan[at.row_phases + first]
        for k in range(1, n):
            late = jnp.maximum(late, plan[at.row_phases + first + k])
        return late

    @pl.when(step == 0)
    def _():
        out[...] = jnp.zeros_like(out)

        @pl.when(latest(0, at.row_tiles) == LAST)
        def _():
            load_panel(LAST, plan[at.me], pieces, panel, sems)

    late = latest(step * GROUP_TILES, GROUP_TILES) == LAST

    @pl.when(late)
    def _():
        build_rows(at, plan, map_ref, panel, left, step)

    @pl.when(~late)
    def _():
        left[...] = early[...]

    across = (((0,), (0,)), ((), ()))
    values = total_ref[...]
    high = values.astype(jnp.bfloat16)
    low = (values - high.astype(jnp.float32)).astype(jnp.bfloat16)
    out[...] += lax.dot_general(left[...], high, across, preferred_element_type=jnp.float32) + lax.dot_general(
        left[...], low, across, preferred_element_type=jnp.float32
    )


def diag_product(at, plan, map3, pieces, early, total):
    rows, width = total.shape
    chunk = GROUP_TILES * TILE
    vmem = pl.BlockSpec(memory_space=pltpu.VMEM)
    hbm = pl.BlockSpec(memory_space=pltpu.HBM)
    block = pl.BlockSpec((chunk, width), lambda i, plan: (i, 0))
    return pl.pallas_call(
        functools.partial(diag_kernel, at, len(pieces)),
        grid_spec=pltpu.PrefetchScalarGridSpec(
            num_scalar_prefetch=1,
            grid=(rows // chunk,),
            in_specs=[block, block, vmem] + [hbm] * len(pieces),
            out_specs=pl.BlockSpec((width, width), lambda i, plan: (0, 0)),
            scratch_shapes=[
                pltpu.VMEM((chunk, width), jnp.bfloat16),
                pltpu.VMEM((map3.shape[0] * LANES, width), jnp.bfloat16),
                pltpu.SemaphoreType.DMA((len(pieces),)),
            ],
        ),
        out_shape=jax.ShapeDtypeStruct((width, width), jnp.float32),
        compiler_params=pltpu.CompilerParams(vmem_limit_bytes=LIMIT),
        cost_estimate=SMALL,
        name="diag_product",
    )(plan, total, early, map3, *pieces)


def second_kernel(plan, low_ref, high_ref, x_in, y_in, low_out, high_out):
    rows = low_ref.shape[0]
    quantized(low_ref[...] + decoded(x_in, rows), low_out)
    quantized(high_ref[...] + decoded(y_in, rows), high_out)


def second_hop(at, plan, total, x_in, y_in):
    half, width = total.shape[0] // 8, total.shape[1]
    coded = x_in.shape[0] // 2
    payload = pl.BlockSpec((coded, width), lambda i, plan: (0, 0))
    return pl.pallas_call(
        second_kernel,
        grid_spec=pltpu.PrefetchScalarGridSpec(
            num_scalar_prefetch=1,
            grid=(1,),
            in_specs=[
                pl.BlockSpec((half, width), lambda i, plan: ((plan[at.me] ^ 2) * 2, 0)),
                pl.BlockSpec((half, width), lambda i, plan: ((plan[at.me] ^ 1) * 2 + 1, 0)),
                payload,
                payload,
            ],
            out_specs=[payload, payload],
        ),
        out_shape=[jax.ShapeDtypeStruct((coded, width), jnp.int16)] * 2,
        compiler_params=pltpu.CompilerParams(vmem_limit_bytes=LIMIT),
        cost_estimate=SMALL,
        name="second_hop",
    )(plan, total, total, x_in, y_in)


def terms_kernel(n, *refs):
    refs[-1][...] = sum((ref[...] for ref in refs[1:n]), refs[0][...])


def added(terms, after):
    vmem = pl.BlockSpec(memory_space=pltpu.VMEM)
    return pl.pallas_call(
        functools.partial(terms_kernel, len(terms)),
        in_specs=[vmem] * len(terms) + [pl.BlockSpec(memory_space=pl.ANY)] * len(after),
        out_specs=vmem,
        out_shape=jax.ShapeDtypeStruct(terms[0].shape, terms[0].dtype),
        compiler_params=pltpu.CompilerParams(vmem_limit_bytes=LIMIT),
        cost_estimate=SMALL,
        name="added",
    )(*terms, *after)


def last_kernel(at, plan, low_ref, high_ref, x_in, y_in, low_in, high_in, map_ref, out_ref):
    me = plan[at.me]
    rows = low_ref.shape[0]
    tiles = rows // TILE
    sums = [
        low_ref[...] + decoded(x_in, rows) + decoded(low_in, rows),
        high_ref[...] + decoded(y_in, rows) + decoded(high_in, rows),
    ]
    for part, value in enumerate(sums):
        for j in range(tiles):
            n = part * tiles + j
            k = me * 2 * tiles + n
            hits = window_hits(map_ref, plan[at.row_begins + k], plan[at.row_base] + k * TILE)
            marked = jnp.max(jnp.where(hits, 1.0, 0.0), axis=1, keepdims=True)
            tile = value[j * TILE:(j + 1) * TILE, :]
            out_ref[n * TILE:(n + 1) * TILE, :] = jnp.where(marked > 0.5, -tile, 0.0)


def last_sum(at, plan, total, x_in, y_in, low_in, high_in, map3):
    half, width = total.shape[0] // 8, total.shape[1]
    coded = low_in.shape[0]

    def block(rows, n):
        return pl.BlockSpec((rows, width), lambda i, plan: (n, 0))

    return pl.pallas_call(
        functools.partial(last_kernel, at),
        grid_spec=pltpu.PrefetchScalarGridSpec(
            num_scalar_prefetch=1,
            grid=(1,),
            in_specs=[
                pl.BlockSpec((half, width), lambda i, plan: (plan[at.me] * 2, 0)),
                pl.BlockSpec((half, width), lambda i, plan: (plan[at.me] * 2 + 1, 0)),
                block(coded, 1), block(coded, 1), block(coded, 0), block(coded, 0),
                pl.BlockSpec(map3.shape, lambda i, plan: (0, 0, 0)),
            ],
            out_specs=block(2 * half, 0),
        ),
        out_shape=jax.ShapeDtypeStruct((2 * half, width), jnp.float32),
        compiler_params=pltpu.CompilerParams(vmem_limit_bytes=LIMIT),
        cost_estimate=SMALL,
        name="last_sum",
    )(plan, total, total, x_in, y_in, low_in, high_in, map3)


def shares(block, axis):
    n = lax.axis_size(axis)
    me = lax.axis_index(axis)
    share = block.shape[0] // n

    def shifted(value, by):
        return lax.ppermute(value, axis, [(i, (i + by) % n) for i in range(n)])

    def part(of):
        return lax.dynamic_slice_in_dim(block, lax.rem(of, n) * share, share, 0)

    arrived = [shifted(part(me + by), by) for by in range(1, n)]
    return [part(me)] + arrived, shifted


def spread_out(mine, shifted, axis):
    n = lax.axis_size(axis)
    me = lax.axis_index(axis)
    share = mine.shape[0]
    whole = jnp.zeros((n * share,) + mine.shape[1:], mine.dtype)
    for by in range(n):
        value = mine if by == 0 else shifted(mine, by)
        whole = lax.dynamic_update_slice_in_dim(whole, value, lax.rem(me - by + n, n) * share, 0)
    return whole


def four_columns(front, panel, row_map, diag_inverse):
    me = lax.axis_index("col")
    rows, cols = front.shape
    own = panel[0]
    half = own.shape[0] // 2
    places = row_map[0]
    map3 = places.reshape(-1, 1, LANES)
    total_rows = places.shape[0]
    at = Layout(rows, cols)

    def partner(value, bit):
        return lax.ppermute(value, "col", [(i, i ^ bit) for i in range(4)])

    def half_of(which):
        return lax.dynamic_slice_in_dim(own, which * half, half, 0)

    high = near_half(me)
    x_near = partner(half_of(high), 1)
    y_far = partner(half_of(1 - high), 2)

    col_base = me * cols
    row_base = lax.axis_index("row") * rows
    marks = jnp.concatenate([
        col_base + TILE * jnp.arange(cols // TILE + 1, dtype=jnp.int32),
        row_base + TILE * jnp.arange(rows // TILE + 1, dtype=jnp.int32),
    ])
    before = jnp.sum(places[None, :] < marks[:, None], axis=1, dtype=jnp.int32)
    place = jnp.stack([me, col_base, row_base]).astype(jnp.int32)
    plan, near, far = make_plan(at, half, total_rows, before, place, own)

    x_far = partner(far, 1)
    y_near = partner(near, 2)
    start = first_strips(at, plan, front, map3, own)
    d_near = partner(x_near, 2)
    d_far = partner(y_far, 1)
    pieces = [own, x_near, y_far]
    total, early = next_strips(at, plan, front, map3, pieces, start)
    pieces += [x_far, y_near, d_near, d_far]
    to_x, to_y, total = last_strips(at, plan, front, map3, pieces, total)
    total = pltpu.with_memory_space_constraint(total, pltpu.HBM)
    from_x = partner(to_x, 1)
    from_y = partner(to_y, 2)
    in_hbm = [pltpu.with_memory_space_constraint(piece, pltpu.HBM) for piece in pieces]
    terms, shifted = shares(diag_product(at, plan, map3, in_hbm, early, total), "row")
    low, high = second_hop(at, plan, total, from_x, from_y)
    mine = sum(terms[1:], terms[0])
    terms = [mine] + [partner(mine, bit) for bit in (1, 2, 3)]
    mine = added(terms, [low])
    low = partner(low, 2)
    high = partner(high, 1)
    diag = diag_inverse[0] + spread_out(mine, shifted, "row")
    offdiag = last_sum(at, plan, total, from_x, from_y, low, high, map3)
    return offdiag[None], diag[None]


def spread_range(padded_rows, padded_places, places, lower, count):
    blk = math.gcd(count, 128)
    nblk = count // blk
    starts = lower + jnp.arange(nblk, dtype=jnp.int32) * blk
    first = jnp.searchsorted(places, starts)

    def window(begin):
        rows = lax.dynamic_slice_in_dim(padded_rows, begin, blk, 0)
        marks = lax.dynamic_slice_in_dim(padded_places, begin, blk, 0)
        return (rows, marks)

    rows, marks = jax.vmap(window)(first)
    target = starts[:, None] + jnp.arange(blk, dtype=jnp.int32)[None, :]
    onehot = marks[:, None, :] == target[:, :, None]
    table = onehot.astype(jnp.bfloat16)
    spread = jnp.einsum("njk,nkw->njw", table, rows, preferred_element_type=jnp.float32)
    hits = jnp.sum(onehot.astype(jnp.float32), axis=2)
    return (spread.astype(jnp.bfloat16).reshape(count, rows.shape[2]), hits.reshape(count))


def any_columns(front_inverse, panel, row_map, diag_inverse):
    row_index = lax.axis_index("row")
    col_index = lax.axis_index("col")
    ncol = lax.axis_size("col")
    front_rows, front_cols = front_inverse.shape
    share = front_rows // ncol
    width = panel.shape[2]
    col_lower = col_index * front_cols
    row_lower = row_index * front_rows
    share_lower = row_lower + col_index * share
    places_all = row_map[0]
    whole_panel = lax.all_gather(panel, "col", axis=1, tiled=True)[0]
    padded_rows = jnp.concatenate([whole_panel, jnp.zeros((128, width), jnp.bfloat16)], axis=0)
    total_front = front_rows * lax.axis_size("row")
    padded_places = jnp.concatenate([places_all, jnp.full((128,), total_front, jnp.int32)], axis=0)
    spread_cols, unused_hits = spread_range(
        padded_rows, padded_places, places_all, col_lower, front_cols
    )
    spread_rows, share_hits = spread_range(
        padded_rows, padded_places, places_all, share_lower, share
    )
    product = lax.psum_scatter(
        jnp.dot(front_inverse, spread_cols, preferred_element_type=jnp.float32),
        "col",
        scatter_dimension=0,
        tiled=True,
    )
    local_terms = jnp.dot(
        spread_rows.astype(jnp.float32).T, product, precision=lax.Precision.HIGHEST
    )
    diag_terms = lax.psum(local_terms, ("row", "col"))
    offdiag = jnp.where(share_hits[:, None] > 0.5, -product, jnp.zeros_like(product))
    diag = diag_inverse[0] + diag_terms
    return (offdiag[None], diag[None])


def solution(mesh):
    return jax.shard_map(
        four_columns if mesh.shape["col"] == 4 else any_columns,
        mesh=mesh,
        in_specs=(P("row", "col"), P("sib", "col", None), P("sib", None), P("sib", None, None)),
        out_specs=(P("sib", ("row", "col"), None), P("sib", None, None)),
        check_vma=False,
    )
```

```python
import functools

import jax
import jax.numpy as jnp
from jax import lax
from jax.experimental import pallas as pl
from jax.experimental.pallas import tpu as pltpu
from jax.sharding import PartitionSpec as P
import math

LANES = 128
TILE = 256
WINDOW = TILE + LANES
STRIP = 2 * TILE
SLOTS = 3
GROUP = 64
STEPS = 256.0
TOP = 32766.0
ROUND = 12582912.0
LIMIT = 40 * 1024 * 1024
FIRST = 3
KERNELS = 4
GROUP_TILES = 4
SMALL = pl.CostEstimate(flops=1000, bytes_accessed=1000, transcendentals=0)
LAST = 3


class Layout:
    def __init__(self, rows, cols):
        self.strips = cols // STRIP
        self.col_tiles = cols // TILE
        self.row_tiles = rows // TILE
        self.counts = 0
        self.lists = KERNELS
        self.col_begins = self.lists + KERNELS * self.strips
        self.row_begins = self.col_begins + self.col_tiles
        self.row_phases = self.row_begins + self.row_tiles
        self.me = self.row_phases + self.row_tiles
        self.col_base = self.me + 1
        self.row_base = self.me + 2
        self.row = self.me + 3
        self.size = self.me + 4


def near_half(shard):
    return 1 - lax.rem(shard, 2)


def arrival(block, me):
    shard = lax.div(block, 2)
    near = lax.rem(block, 2) == near_half(shard)
    away = shard ^ me
    beside = jnp.where(near == (away == 1), 1, 3)
    return jnp.where(away == 0, 0, jnp.where(away == 3, 2, beside))


def plan_kernel(at, half, total_rows, before, place, plan):
    me = place[0]

    def phase(first, last):
        start = arrival(lax.div(first, half), me)
        end = arrival(lax.div(last - 1, half), me)
        return jnp.maximum(start, end)

    def begin(first):
        return jnp.minimum(lax.div(first, LANES) * LANES, total_rows - WINDOW)

    for i in range(KERNELS * at.strips):
        plan[at.lists + i] = 0
    counts = [jnp.int32(0)] * KERNELS
    per = STRIP // TILE
    for s in range(at.strips):
        first, last = before[s * per], before[(s + 1) * per]
        when = phase(first, last)
        some = last > first
        taken = jnp.bool_(False)
        for j in range(KERNELS):
            fits = some & (when <= j) & ~taken
            if j == 0:
                fits = fits & (counts[j] < FIRST)

            @pl.when(fits)
            def _():
                plan[at.lists + j * at.strips + counts[j]] = s

            counts[j] = counts[j] + jnp.where(fits, 1, 0)
            taken = taken | fits
    for j in range(KERNELS):
        plan[at.counts + j] = counts[j]
    for k in range(at.col_tiles):
        plan[at.col_begins + k] = begin(before[k])
    base = at.col_tiles + 1
    for k in range(at.row_tiles):
        first, last = before[base + k], before[base + k + 1]
        plan[at.row_begins + k] = begin(first)
        plan[at.row_phases + k] = jnp.where(last > first, phase(first, last), 0)
    for i in range(4):
        plan[at.me + i] = place[i]


def make_plan(at, half, total_rows, before, place):
    smem = pl.BlockSpec(memory_space=pltpu.SMEM)
    return pl.pallas_call(
        functools.partial(plan_kernel, at, half, total_rows),
        in_specs=[smem, smem],
        out_specs=smem,
        out_shape=jax.ShapeDtypeStruct((at.size,), jnp.int32),
        compiler_params=pltpu.CompilerParams(vmem_limit_bytes=LIMIT),
        cost_estimate=SMALL,
        name="plan",
    )(before, place)


def halves_kernel(which, own, first, second, sems):
    half = first.shape[0]
    copies = [
        pltpu.make_async_copy(own.at[pl.ds(pl.multiple_of(part * half, LANES), half)], out, sems.at[n])
        for n, (part, out) in enumerate(((which[0], first), (1 - which[0], second)))
    ]
    for copy in copies:
        copy.start()
    for copy in copies:
        copy.wait()


def halves(which, own):
    piece = pltpu.VMEM((own.shape[0] // 2, own.shape[1]), own.dtype)
    vmem = pl.BlockSpec(memory_space=pltpu.VMEM)
    return pl.pallas_call(
        halves_kernel,
        in_specs=[pl.BlockSpec(memory_space=pltpu.SMEM), pl.BlockSpec(memory_space=pltpu.HBM)],
        out_specs=[vmem, vmem],
        out_shape=[piece, piece],
        scratch_shapes=[pltpu.SemaphoreType.DMA((2,))],
        compiler_params=pltpu.CompilerParams(vmem_limit_bytes=LIMIT),
        cost_estimate=SMALL,
        name="halves",
    )(which, own)


def window_hits(map_ref, begin, target):
    first = lax.div(begin, LANES)
    row = jnp.concatenate([map_ref[first + j] for j in range(WINDOW // LANES)], axis=1)
    wanted = lax.broadcasted_iota(jnp.int32, (TILE, WINDOW), 0) + target
    return wanted == row


def spread_tile(panel_ref, map_ref, begin, target):
    table = jnp.where(window_hits(map_ref, begin, target), 1.0, 0.0).astype(jnp.bfloat16)
    rows = panel_ref[pl.ds(pl.multiple_of(begin, LANES), WINDOW), :]
    return jnp.dot(table, rows, preferred_element_type=jnp.float32).astype(jnp.bfloat16)


def strip_tile(at, s, plan, map_ref, panel, strip):
    per = STRIP // TILE
    for t in range(per):
        k = s * per + t
        strip[t * TILE:(t + 1) * TILE, :] = spread_tile(
            panel, map_ref, plan[at.col_begins + k], plan[at.col_base] + k * TILE
        )


def half_block(shard, near):
    return shard * 2 + (near_half(shard) if near else 1 - near_half(shard))


def piece_blocks(me):
    return [
        me,
        half_block(me ^ 1, True), half_block(me ^ 2, False),
        half_block(me ^ 3, True), half_block(me ^ 3, False),
        half_block(me ^ 1, False), half_block(me ^ 2, True),
    ]


def panel_copies(me, pieces, panel, sems):
    copies = []
    for n, (piece, block) in enumerate(zip(pieces, piece_blocks(me))):
        size = piece.shape[0]
        copies.append(
            pltpu.make_async_copy(piece, panel.at[pl.ds(pl.multiple_of(block * size, LANES), size)], sems.at[n])
        )
    return copies


def clear_panel(step, me, half, panel):
    for block in range(panel.shape[0] // half):
        @pl.when(arrival(jnp.int32(block), me) > step)
        def _():
            panel[block * half:(block + 1) * half, :] = jnp.zeros((half, panel.shape[1]), panel.dtype)


def row_tile(at, k, plan, map_ref, panel):
    return spread_tile(panel, map_ref, plan[at.row_begins + k], plan[at.row_base] + k * TILE)


def build_rows(at, first, last, plan, map_ref, panel, tiles, spread, sems):
    def written(k):
        return pltpu.make_async_copy(
            tiles.at[k], spread.at[pl.ds(pl.multiple_of(k * TILE, TILE), TILE)], sems.at[0]
        )

    def chosen(k):
        phase = plan[at.row_phases + k]
        return (phase >= first) & (phase <= last)

    @pl.loop(0, at.row_tiles)
    def _(k):
        @pl.when(chosen(k))
        def _():
            tiles[k] = row_tile(at, k, plan, map_ref, panel)
            written(k).start()

    @pl.loop(0, at.row_tiles)
    def _(k):
        pl.when(chosen(k))(lambda: written(k).wait())


def fetched(at, j, plan, front, fronts, sems, i):
    s = plan[at.lists + j * at.strips + i]
    slot = lax.rem(i, SLOTS)
    return pltpu.make_async_copy(
        front.at[:, pl.ds(pl.multiple_of(s * STRIP, STRIP), STRIP)], fronts.at[slot], sems.at[slot]
    )


def strips_begin(at, j, plan, front, fronts, sems, i):
    @pl.when(i < plan[at.counts + j])
    def _():
        fetched(at, j, plan, front, fronts, sems, jnp.int32(i)).start()


def begin(at, j, plan, front, fronts, sems, pieces, panel, own_sems, arriving):
    copies = panel_copies(plan[at.me], pieces, panel, own_sems)
    for copy in copies:
        copy.start()
    strips_begin(at, j, plan, front, fronts, sems, 0)
    for copy in arriving:
        copy.start()
    for i in range(1, SLOTS - 1):
        strips_begin(at, j, plan, front, fronts, sems, i)
    if j < LAST:
        clear_panel(j, plan[at.me], pieces[0].shape[0] // 2, panel)
    for copy in copies:
        copy.wait()


def strips_loop(at, j, plan, front, fronts, sems, map_ref, panel, strips, total):
    count = plan[at.counts + j]
    listed = at.lists + j * at.strips

    @pl.when(count > 0)
    def _():
        strip_tile(at, plan[listed], plan, map_ref, panel, strips.at[0])

    @pl.loop(0, count)
    def _(i):
        @pl.when(i + SLOTS - 1 < count)
        def _():
            fetched(at, j, plan, front, fronts, sems, i + SLOTS - 1).start()

        now = lax.rem(i, 2)
        following = plan[listed + jnp.minimum(i + 1, count - 1)]
        fetched(at, j, plan, front, fronts, sems, i).wait()
        total[...] += jnp.dot(fronts[lax.rem(i, SLOTS)], strips[now], preferred_element_type=jnp.float32)
        strip_tile(at, following, plan, map_ref, panel, strips.at[1 - now])


def first_kernel(at, plan, front, map_ref, own, out, total, fronts, panel, strips, sems, own_sems):
    begin(at, 0, plan, front, fronts, sems, [own], panel, own_sems, [])
    total[...] = jnp.zeros_like(total)
    strips_loop(at, 0, plan, front, fronts, sems, map_ref, panel, strips, total)
    leaving = pltpu.make_async_copy(total, out, own_sems.at[0])
    leaving.start()
    leaving.wait()


def next_kernel(at, j, n_pieces, *refs):
    plan, front, map_ref = refs[:3]
    pieces = refs[3:3 + n_pieces]
    start = refs[3 + n_pieces]
    total, spread, tiles, fronts, panel, strips, sems, own_sems = refs[-8:]
    first = 0 if j == 1 else j
    wanted = plan[at.counts + j] > 0
    for k in range(at.row_tiles):
        wanted = wanted | ((plan[at.row_phases + k] >= first) & (plan[at.row_phases + k] <= j))
    arriving = [pltpu.make_async_copy(start, total, own_sems.at[n_pieces])] if j == 1 else []

    @pl.when(wanted)
    def _():
        begin(at, j, plan, front, fronts, sems, pieces, panel, own_sems, arriving)

    if j == 1:
        @pl.when(~wanted)
        def _():
            arriving[0].start()

        arriving[0].wait()

    @pl.when(wanted)
    def _():
        strips_loop(at, j, plan, front, fronts, sems, map_ref, panel, strips, total)
        build_rows(at, first, j, plan, map_ref, panel, tiles, spread, own_sems)


def strips_call(kernel, at, plan, front, map3, others, out_specs, out_shape, scratch, expected, name, carried=()):
    rows = front.shape[0]
    width = others[0].shape[1]
    vmem = pl.BlockSpec(memory_space=pltpu.VMEM)
    smem = pl.BlockSpec(memory_space=pltpu.SMEM)
    hbm = pl.BlockSpec(memory_space=pltpu.HBM)
    return pl.pallas_call(
        functools.partial(kernel, at),
        in_specs=[smem, hbm, vmem] + [hbm] * len(others) + [vmem, hbm][:len(carried)],
        out_specs=out_specs,
        scratch_shapes=scratch + [
            pltpu.VMEM((SLOTS, rows, STRIP), jnp.bfloat16),
            pltpu.VMEM((map3.shape[0] * LANES, width), jnp.bfloat16),
            pltpu.VMEM((2, STRIP, width), jnp.bfloat16),
            pltpu.SemaphoreType.DMA((SLOTS,)),
            pltpu.SemaphoreType.DMA((len(others) + 2,)),
        ],
        out_shape=out_shape,
        input_output_aliases={3 + len(others) + n: n for n in range(len(carried))},
        compiler_params=pltpu.CompilerParams(vmem_limit_bytes=LIMIT),
        cost_estimate=pl.CostEstimate(
            flops=8 * rows * STRIP * width * expected, bytes_accessed=8 * rows * STRIP * expected, transcendentals=0
        ),
        name=name,
    )(plan, front, map3, *others, *carried)


def first_strips(at, plan, front, map3, own):
    shape = front.shape[0], own.shape[1]
    return strips_call(
        first_kernel, at, plan, front, map3, [own], [pl.BlockSpec(memory_space=pltpu.HBM)],
        [pltpu.HBM(shape, jnp.float32)], [pltpu.VMEM(shape, jnp.float32)], FIRST, "strips_0",
    )[0]


def next_strips(at, j, plan, front, map3, pieces, start, spread=None):
    rows, width = start.shape
    return strips_call(
        lambda at, *refs: next_kernel(at, j, len(pieces), *refs), at, plan, front, map3,
        pieces + [start] * (j == 1), [pl.BlockSpec(memory_space=pltpu.VMEM), pl.BlockSpec(memory_space=pltpu.HBM)],
        [pltpu.VMEM(start.shape, start.dtype), pltpu.HBM((rows, width), jnp.bfloat16)],
        [pltpu.VMEM((at.row_tiles, TILE, width), jnp.bfloat16)], at.strips, f"strips_{j}", [start, spread][:2 * (j == 2)],
    )


def quantized(values, out_ref):
    rows, width = values.shape[0], values.shape[1]
    codes = []
    for g in range(rows // GROUP):
        part = values[g * GROUP:(g + 1) * GROUP, :]
        most = jnp.max(jnp.abs(part), axis=0, keepdims=True)
        code = jnp.clip(jnp.ceil(jnp.log2(jnp.maximum(most, 1e-30)) * STEPS) + 1.0, -32000.0, 32000.0)
        inverse = TOP / jnp.exp2(code * (1.0 / STEPS))
        whole = ((part * inverse + ROUND) - ROUND).astype(jnp.int32)
        out_ref[g * GROUP:(g + 1) * GROUP, :] = whole.astype(jnp.int16)
        codes.append(code)
    codes.append(jnp.zeros((out_ref.shape[0] - rows - len(codes), width), jnp.float32))
    tail = jnp.concatenate(codes, axis=0).astype(jnp.int32)
    out_ref[rows:, :] = tail.astype(jnp.int16)


def coded_rows(rows):
    return rows + (rows // GROUP + 15) // 16 * 16


def decoded(ref, rows):
    codes = ref[rows:, :].astype(jnp.int32).astype(jnp.float32)
    scales = jnp.exp2(codes * (1.0 / STEPS)) * (1.0 / TOP)
    parts = []
    for g in range(rows // GROUP):
        part = ref[g * GROUP:(g + 1) * GROUP, :].astype(jnp.int32).astype(jnp.float32)
        parts.append(part * scales[g:g + 1, :])
    return jnp.concatenate(parts, axis=0)


def part_of(total, which, part):
    half = total.shape[0] // 8
    return total[pl.ds(pl.multiple_of((which * 2 + part) * half, half), half), :]


def last_strips_kernel(at, n_pieces, *refs):
    plan, front, map_ref = refs[:3]
    pieces = refs[3:3 + n_pieces]
    total, x_out, y_out, written, fronts, panel, strips, sems, own_sems = refs[4 + n_pieces:]
    me = plan[at.me]
    j = KERNELS - 1

    @pl.when(plan[at.counts + j] > 0)
    def _():
        begin(at, j, plan, front, fronts, sems, pieces, panel, own_sems, [])
        strips_loop(at, j, plan, front, fronts, sems, map_ref, panel, strips, total)

    copy = pltpu.make_async_copy(total, written, own_sems.at[0])
    copy.start()
    coded = x_out.shape[0] // 2
    quantized(part_of(total, me ^ 3, 0), x_out.at[:coded])
    quantized(part_of(total, me ^ 1, 0), x_out.at[coded:])
    quantized(part_of(total, me ^ 3, 1), y_out.at[:coded])
    quantized(part_of(total, me ^ 2, 1), y_out.at[coded:])
    copy.wait()


def last_strips(at, plan, front, map3, pieces, total):
    rows, width = total.shape
    coded = coded_rows(rows // 8)
    vmem = pl.BlockSpec(memory_space=pltpu.VMEM)
    smem = pl.BlockSpec(memory_space=pltpu.SMEM)
    hbm = pl.BlockSpec(memory_space=pltpu.HBM)
    return pl.pallas_call(
        functools.partial(last_strips_kernel, at, len(pieces)),
        in_specs=[smem, hbm, vmem] + [hbm] * len(pieces) + [vmem],
        out_specs=[vmem] * 3 + [hbm],
        scratch_shapes=[
            pltpu.VMEM((SLOTS, rows, STRIP), jnp.bfloat16),
            pltpu.VMEM((map3.shape[0] * LANES, width), jnp.bfloat16),
            pltpu.VMEM((2, STRIP, width), jnp.bfloat16),
            pltpu.SemaphoreType.DMA((SLOTS,)),
            pltpu.SemaphoreType.DMA((len(pieces),)),
        ],
        out_shape=[
            pltpu.VMEM(total.shape, total.dtype),
        ] + [jax.ShapeDtypeStruct((2 * coded, width), jnp.int16)] * 2 + [pltpu.HBM(total.shape, total.dtype)],
        input_output_aliases={3 + len(pieces): 0},
        compiler_params=pltpu.CompilerParams(vmem_limit_bytes=LIMIT),
        cost_estimate=SMALL,
        name="last_strips",
    )(plan, front, map3, *pieces, total)[1:]


def diag_kernel(at, n_pieces, *refs):
    plan, total, early, map_ref = refs[:4]
    pieces = refs[4:4 + n_pieces]
    outs = refs[4 + n_pieces:-6]
    sums, values, lefts, panel, block_sems, sems = refs[-6:]
    groups, rows = values.shape[:2]
    row_tiles = rows // TILE

    def late(k):
        return plan[at.row_phases + k] == LAST

    def some_late(first, n):
        found = late(first)
        for k in range(1, n):
            found = found | late(first + k)
        return found

    def blocks(group):
        place = pl.ds(pl.multiple_of(group * rows, rows), rows)
        return [
            pltpu.make_async_copy(total.at[place], values.at[group], block_sems.at[0, group]),
            pltpu.make_async_copy(early.at[place], lefts.at[group], block_sems.at[1, group]),
        ]

    def add(group):
        high = values[group].astype(jnp.bfloat16)
        low = (values[group] - high.astype(jnp.float32)).astype(jnp.bfloat16)
        sums[...] += lax.dot_general(
            lefts[group], jnp.concatenate([high, low], axis=1), (((0,), (0,)), ((), ())),
            preferred_element_type=jnp.float32,
        )

    for group in range(groups):
        for copy in blocks(group):
            copy.start()
    any_late = some_late(0, at.row_tiles)
    copies = panel_copies(plan[at.me], pieces, panel, sems)

    @pl.when(any_late)
    def _():
        for copy in copies:
            copy.start()

    sums[...] = jnp.zeros_like(sums)

    @pl.loop(0, groups)
    def _(group):
        for copy in blocks(group):
            copy.wait()

        @pl.when(~some_late(group * row_tiles, row_tiles))
        def _():
            add(group)

    @pl.when(any_late)
    def _():
        for copy in copies:
            copy.wait()

        @pl.loop(0, groups)
        def _(group):
            @pl.when(some_late(group * row_tiles, row_tiles))
            def _():
                for t in range(row_tiles):
                    k = group * row_tiles + t

                    @pl.when(late(k))
                    def _():
                        lefts[group, t * TILE:(t + 1) * TILE, :] = row_tile(at, k, plan, map_ref, panel)

                add(group)

    share, width = outs[0].shape
    for by, out in enumerate(outs):
        place = pl.ds(pl.multiple_of(lax.rem(plan[at.row] + by, len(outs)) * share, share), share)
        out[...] = sums[place, :width] + sums[place, width:]


def diag_product(at, plan, map3, pieces, early, total, shares):
    rows, width = total.shape
    chunk = GROUP_TILES * TILE
    vmem = pl.BlockSpec(memory_space=pltpu.VMEM)
    hbm = pl.BlockSpec(memory_space=pltpu.HBM)
    return pl.pallas_call(
        functools.partial(diag_kernel, at, len(pieces)),
        in_specs=[pl.BlockSpec(memory_space=pltpu.SMEM), hbm, hbm, vmem] + [hbm] * len(pieces),
        out_specs=[vmem] * shares,
        out_shape=[jax.ShapeDtypeStruct((width // shares, width), jnp.float32)] * shares,
        scratch_shapes=[
            pltpu.VMEM((width, 2 * width), jnp.float32),
            pltpu.VMEM((rows // chunk, chunk, width), jnp.float32),
            pltpu.VMEM((rows // chunk, chunk, width), jnp.bfloat16),
            pltpu.VMEM((map3.shape[0] * LANES, width), jnp.bfloat16),
            pltpu.SemaphoreType.DMA((2, rows // chunk)),
            pltpu.SemaphoreType.DMA((len(pieces),)),
        ],
        compiler_params=pltpu.CompilerParams(vmem_limit_bytes=LIMIT),
        cost_estimate=SMALL,
        name="diag_product",
    )(plan, total, early, map3, *pieces)


def second_kernel(plan, low_ref, high_ref, x_in, y_in, *refs):
    terms, (low_out, high_out, sum_out) = refs[:-3], refs[-3:]
    rows = low_ref.shape[0]
    quantized(low_ref[...] + decoded(x_in, rows), low_out)
    quantized(high_ref[...] + decoded(y_in, rows), high_out)
    sum_out[...] = sum((term[...] for term in terms[1:]), terms[0][...])


def second_hop(at, plan, total, x_in, y_in, terms):
    half, width = total.shape[0] // 8, total.shape[1]
    coded = x_in.shape[0] // 2
    payload = pl.BlockSpec((coded, width), lambda i, plan: (0, 0))
    term = pl.BlockSpec(terms[0].shape, lambda i, plan: (0, 0))
    return pl.pallas_call(
        second_kernel,
        grid_spec=pltpu.PrefetchScalarGridSpec(
            num_scalar_prefetch=1,
            grid=(1,),
            in_specs=[
                pl.BlockSpec((half, width), lambda i, plan: ((plan[at.me] ^ 2) * 2, 0)),
                pl.BlockSpec((half, width), lambda i, plan: ((plan[at.me] ^ 1) * 2 + 1, 0)),
                payload,
                payload,
            ] + [term] * len(terms),
            out_specs=[payload, payload, term],
        ),
        out_shape=[jax.ShapeDtypeStruct((coded, width), jnp.int16)] * 2
        + [jax.ShapeDtypeStruct(terms[0].shape, jnp.float32)],
        compiler_params=pltpu.CompilerParams(vmem_limit_bytes=LIMIT),
        cost_estimate=SMALL,
        name="second_hop",
    )(plan, total, total, x_in, y_in, *terms)


def gate_kernel(n, *refs):
    sems = refs[-1]
    copies = [
        pltpu.make_async_copy(source, out, sems.at[i]) for i, (source, out) in enumerate(zip(refs[:n], refs[n:2 * n]))
    ]
    for copy in copies:
        copy.start()
    for copy in copies:
        copy.wait()


def gated(values):
    return pl.pallas_call(
        functools.partial(gate_kernel, len(values)),
        in_specs=[pl.BlockSpec(memory_space=pl.ANY)] * len(values),
        out_specs=[pl.BlockSpec(memory_space=pltpu.VMEM)] * len(values),
        out_shape=[pltpu.VMEM(value.shape, value.dtype) for value in values],
        scratch_shapes=[pltpu.SemaphoreType.DMA((len(values),))],
        compiler_params=pltpu.CompilerParams(vmem_limit_bytes=LIMIT),
        cost_estimate=SMALL,
        name="gated",
    )(*values)


def last_kernel(at, plan, low_ref, high_ref, x_in, y_in, low_in, high_in, map_ref, out_ref):
    me = plan[at.me]
    rows = low_ref.shape[0]
    tiles = rows // TILE
    sums = [
        low_ref[...] + decoded(x_in, rows) + decoded(low_in, rows),
        high_ref[...] + decoded(y_in, rows) + decoded(high_in, rows),
    ]
    for part, value in enumerate(sums):
        for j in range(tiles):
            n = part * tiles + j
            k = me * 2 * tiles + n
            hits = window_hits(map_ref, plan[at.row_begins + k], plan[at.row_base] + k * TILE)
            marked = jnp.max(jnp.where(hits, 1.0, 0.0), axis=1, keepdims=True)
            tile = value[j * TILE:(j + 1) * TILE, :]
            out_ref[n * TILE:(n + 1) * TILE, :] = jnp.where(marked > 0.5, -tile, 0.0)


def last_sum(at, plan, total, x_in, y_in, low_in, high_in, map3):
    half, width = total.shape[0] // 8, total.shape[1]
    first = pl.BlockSpec(low_in.shape, lambda i, plan: (0, 0))
    second = pl.BlockSpec(low_in.shape, lambda i, plan: (1, 0))
    return pl.pallas_call(
        functools.partial(last_kernel, at),
        grid_spec=pltpu.PrefetchScalarGridSpec(
            num_scalar_prefetch=1,
            grid=(1,),
            in_specs=[
                pl.BlockSpec((half, width), lambda i, plan: (plan[at.me] * 2, 0)),
                pl.BlockSpec((half, width), lambda i, plan: (plan[at.me] * 2 + 1, 0)),
                second, second, first, first,
                pl.BlockSpec(map3.shape, lambda i, plan: (0, 0, 0)),
            ],
            out_specs=pl.BlockSpec((2 * half, width), lambda i, plan: (0, 0)),
        ),
        out_shape=pltpu.HBM((2 * half, width), jnp.float32),
        compiler_params=pltpu.CompilerParams(vmem_limit_bytes=LIMIT),
        cost_estimate=SMALL,
        name="last_sum",
    )(plan, total, total, x_in, y_in, low_in, high_in, map3)


def together_kernel(at, plan, start, *refs):
    shares, out = refs[:-1], refs[-1]
    for by, share in enumerate(shares):
        size = share.shape[0]
        place = pl.ds(pl.multiple_of(lax.rem(plan[at.row] - by + len(shares), len(shares)) * size, size), size)
        out[place, :] = start[place, :] + share[...]


def together(at, plan, start, shares):
    vmem = pl.BlockSpec(memory_space=pltpu.VMEM)
    return pl.pallas_call(
        functools.partial(together_kernel, at),
        in_specs=[pl.BlockSpec(memory_space=pltpu.SMEM), vmem] + [vmem] * len(shares),
        out_specs=vmem,
        out_shape=jax.ShapeDtypeStruct(start.shape, start.dtype),
        compiler_params=pltpu.CompilerParams(vmem_limit_bytes=LIMIT),
        cost_estimate=SMALL,
        name="together",
    )(plan, start, *shares)


def four_columns(front, panel, row_map, diag_inverse):
    me = lax.axis_index("col")
    rows, cols = front.shape
    own = panel[0]
    half = own.shape[0] // 2
    places = row_map[0]
    map3 = places.reshape(-1, 1, LANES)
    total_rows = places.shape[0]
    at = Layout(rows, cols)

    def partner(value, bit):
        return lax.ppermute(value, "col", [(i, i ^ bit) for i in range(4)])

    def shifted(value, by):
        n = lax.axis_size("row")
        return lax.ppermute(value, "row", [(i, (i + by) % n) for i in range(n)])

    def in_hbm(value):
        return pltpu.with_memory_space_constraint(value, pltpu.HBM)

    own = in_hbm(own)
    near, far = halves(near_half(me).reshape(1), own)
    x_near = partner(near, 1)
    y_far = partner(far, 2)

    col_base = me * cols
    row_base = lax.axis_index("row") * rows
    marks = jnp.concatenate([
        col_base + TILE * jnp.arange(cols // TILE + 1, dtype=jnp.int32),
        row_base + TILE * jnp.arange(rows // TILE + 1, dtype=jnp.int32),
    ])
    before = jnp.sum(places[None, :] < marks[:, None], axis=1, dtype=jnp.int32)
    place = jnp.stack([me, col_base, row_base, lax.axis_index("row")]).astype(jnp.int32)
    plan = make_plan(at, half, total_rows, before, place)

    pieces = [own]
    start = first_strips(at, plan, front, map3, own)
    far, near, x_on, y_on = gated([far, near, x_near, y_far])
    d_near = partner(x_on, 2)
    d_far = partner(y_on, 1)
    x_far = partner(far, 1)
    y_near = partner(near, 2)
    pieces += [x_near, y_far]
    total, early = next_strips(at, 1, plan, front, map3, pieces, in_hbm(start))
    pieces += [d_near, d_far]
    total, early = next_strips(at, 2, plan, front, map3, pieces, total, early)
    pieces += [x_far, y_near]
    to_x, to_y, total = last_strips(at, plan, front, map3, pieces, total)

    total = in_hbm(total)
    from_x, from_y = partner(to_x, 1), partner(to_y, 2)
    n = lax.axis_size("row")
    terms = diag_product(at, plan, map3, [in_hbm(piece) for piece in pieces], in_hbm(early), total, n)
    mine = sum((shifted(terms[by], by) for by in range(1, n)), terms[0])
    terms = [mine] + [partner(mine, bit) for bit in (1, 2, 3)]
    low, high, mine = second_hop(at, plan, total, from_x, from_y, terms)
    low = partner(low, 2)
    high = partner(high, 1)
    offdiag = last_sum(at, plan, total, from_x, from_y, low, high, map3)
    diag = together(at, plan, diag_inverse[0], [mine] + [shifted(mine, by) for by in range(1, n)])
    return offdiag[None], diag[None]


def spread_range(padded_rows, padded_places, places, lower, count):
    blk = math.gcd(count, 128)
    nblk = count // blk
    starts = lower + jnp.arange(nblk, dtype=jnp.int32) * blk
    first = jnp.searchsorted(places, starts)

    def window(begin):
        rows = lax.dynamic_slice_in_dim(padded_rows, begin, blk, 0)
        marks = lax.dynamic_slice_in_dim(padded_places, begin, blk, 0)
        return (rows, marks)

    rows, marks = jax.vmap(window)(first)
    target = starts[:, None] + jnp.arange(blk, dtype=jnp.int32)[None, :]
    onehot = marks[:, None, :] == target[:, :, None]
    table = onehot.astype(jnp.bfloat16)
    spread = jnp.einsum("njk,nkw->njw", table, rows, preferred_element_type=jnp.float32)
    hits = jnp.sum(onehot.astype(jnp.float32), axis=2)
    return (spread.astype(jnp.bfloat16).reshape(count, rows.shape[2]), hits.reshape(count))


def any_columns(front_inverse, panel, row_map, diag_inverse):
    row_index = lax.axis_index("row")
    col_index = lax.axis_index("col")
    ncol = lax.axis_size("col")
    front_rows, front_cols = front_inverse.shape
    share = front_rows // ncol
    width = panel.shape[2]
    col_lower = col_index * front_cols
    row_lower = row_index * front_rows
    share_lower = row_lower + col_index * share
    places_all = row_map[0]
    whole_panel = lax.all_gather(panel, "col", axis=1, tiled=True)[0]
    padded_rows = jnp.concatenate([whole_panel, jnp.zeros((128, width), jnp.bfloat16)], axis=0)
    total_front = front_rows * lax.axis_size("row")
    padded_places = jnp.concatenate([places_all, jnp.full((128,), total_front, jnp.int32)], axis=0)
    spread_cols, unused_hits = spread_range(
        padded_rows, padded_places, places_all, col_lower, front_cols
    )
    spread_rows, share_hits = spread_range(
        padded_rows, padded_places, places_all, share_lower, share
    )
    product = lax.psum_scatter(
        jnp.dot(front_inverse, spread_cols, preferred_element_type=jnp.float32),
        "col",
        scatter_dimension=0,
        tiled=True,
    )
    local_terms = jnp.dot(
        spread_rows.astype(jnp.float32).T, product, precision=lax.Precision.HIGHEST
    )
    diag_terms = lax.psum(local_terms, ("row", "col"))
    offdiag = jnp.where(share_hits[:, None] > 0.5, -product, jnp.zeros_like(product))
    diag = diag_inverse[0] + diag_terms
    return (offdiag[None], diag[None])


def solution(mesh):
    return jax.shard_map(
        four_columns if mesh.shape["col"] == 4 else any_columns,
        mesh=mesh,
        in_specs=(P("row", "col"), P("sib", "col", None), P("sib", None), P("sib", None, None)),
        out_specs=(P("sib", ("row", "col"), None), P("sib", None, None)),
        check_vma=False,
    )
```

```python
import functools

import jax
import jax.numpy as jnp
from jax import lax
from jax.experimental import pallas as pl
from jax.experimental.pallas import tpu as pltpu
from jax.sharding import PartitionSpec as P
import math

LANES = 128
TILE = 256
WINDOW = TILE + LANES
STRIP = 2 * TILE
SLOTS = 3
GROUP = 64
STEPS = 256.0
TOP = 32766.0
ROUND = 12582912.0
LIMIT = 38 * 1024 * 1024
FIRST = 3
KERNELS = 4
GROUP_TILES = 4
NEW = ((0, 1), (0, 3), (3, 5), (5, 7))
SMALL = pl.CostEstimate(flops=1000, bytes_accessed=1000, transcendentals=0)
LAST = 3


class Layout:
    def __init__(self, rows, cols):
        self.strips = cols // STRIP
        self.col_tiles = cols // TILE
        self.row_tiles = rows // TILE
        self.counts = 0
        self.lists = KERNELS
        self.col_begins = self.lists + KERNELS * self.strips
        self.row_begins = self.col_begins + self.col_tiles
        self.row_phases = self.row_begins + self.row_tiles
        self.me = self.row_phases + self.row_tiles
        self.col_base = self.me + 1
        self.row_base = self.me + 2
        self.row = self.me + 3
        self.size = self.me + 4


def near_half(shard):
    return 1 - lax.rem(shard, 2)


def arrival(block, me):
    shard = lax.div(block, 2)
    near = lax.rem(block, 2) == near_half(shard)
    away = shard ^ me
    beside = jnp.where(near == (away == 1), 1, 3)
    return jnp.where(away == 0, 0, jnp.where(away == 3, 2, beside))


def plan_kernel(at, half, total_rows, before, place, plan):
    me = place[0]

    def phase(first, last):
        start = arrival(lax.div(first, half), me)
        end = arrival(lax.div(last - 1, half), me)
        return jnp.maximum(start, end)

    def begin(first):
        return jnp.minimum(lax.div(first, LANES) * LANES, total_rows - WINDOW)

    for i in range(KERNELS * at.strips):
        plan[at.lists + i] = 0
    counts = [jnp.int32(0)] * KERNELS
    per = STRIP // TILE
    for s in range(at.strips):
        first, last = before[s * per], before[(s + 1) * per]
        when = phase(first, last)
        some = last > first
        taken = jnp.bool_(False)
        for j in range(KERNELS):
            fits = some & (when <= j) & ~taken
            if j == 0:
                fits = fits & (counts[j] < FIRST)

            @pl.when(fits)
            def _():
                plan[at.lists + j * at.strips + counts[j]] = s

            counts[j] = counts[j] + jnp.where(fits, 1, 0)
            taken = taken | fits
    for j in range(KERNELS):
        plan[at.counts + j] = counts[j]
    for k in range(at.col_tiles):
        plan[at.col_begins + k] = begin(before[k])
    base = at.col_tiles + 1
    for k in range(at.row_tiles):
        first, last = before[base + k], before[base + k + 1]
        plan[at.row_begins + k] = begin(first)
        plan[at.row_phases + k] = jnp.where(last > first, phase(first, last), 0)
    for i in range(4):
        plan[at.me + i] = place[i]


def make_plan(at, half, total_rows, before, place):
    smem = pl.BlockSpec(memory_space=pltpu.SMEM)
    return pl.pallas_call(
        functools.partial(plan_kernel, at, half, total_rows),
        in_specs=[smem, smem],
        out_specs=smem,
        out_shape=jax.ShapeDtypeStruct((at.size,), jnp.int32),
        compiler_params=pltpu.CompilerParams(vmem_limit_bytes=LIMIT),
        cost_estimate=SMALL,
        name="plan",
    )(before, place)


def halves_kernel(which, own, first, second, sems):
    half = first.shape[0]
    copies = [
        pltpu.make_async_copy(own.at[pl.ds(pl.multiple_of(part * half, LANES), half)], out, sems.at[n])
        for n, (part, out) in enumerate(((which[0], first), (1 - which[0], second)))
    ]
    for copy in copies:
        copy.start()
    for copy in copies:
        copy.wait()


def halves(which, own):
    piece = pltpu.VMEM((own.shape[0] // 2, own.shape[1]), own.dtype)
    vmem = pl.BlockSpec(memory_space=pltpu.VMEM)
    return pl.pallas_call(
        halves_kernel,
        in_specs=[pl.BlockSpec(memory_space=pltpu.SMEM), pl.BlockSpec(memory_space=pltpu.HBM)],
        out_specs=[vmem, vmem],
        out_shape=[piece, piece],
        scratch_shapes=[pltpu.SemaphoreType.DMA((2,))],
        compiler_params=pltpu.CompilerParams(vmem_limit_bytes=LIMIT),
        cost_estimate=SMALL,
        name="halves",
    )(which, own)


def window_hits(map_ref, begin, target):
    first = lax.div(begin, LANES)
    row = jnp.concatenate([map_ref[first + j] for j in range(WINDOW // LANES)], axis=1)
    wanted = lax.broadcasted_iota(jnp.int32, (TILE, WINDOW), 0) + target
    return wanted == row


def spread_tile(panel_ref, map_ref, begin, target):
    table = jnp.where(window_hits(map_ref, begin, target), 1.0, 0.0).astype(jnp.bfloat16)
    rows = panel_ref[pl.ds(pl.multiple_of(begin, LANES), WINDOW), :]
    return jnp.dot(table, rows, preferred_element_type=jnp.float32).astype(jnp.bfloat16)


def strip_tile(at, s, plan, map_ref, panel, strip):
    per = STRIP // TILE
    for t in range(per):
        k = s * per + t
        strip[t * TILE:(t + 1) * TILE, :] = spread_tile(
            panel, map_ref, plan[at.col_begins + k], plan[at.col_base] + k * TILE
        )


def half_block(shard, near):
    return shard * 2 + (near_half(shard) if near else 1 - near_half(shard))


def piece_blocks(me):
    return [
        me,
        half_block(me ^ 1, True), half_block(me ^ 2, False),
        half_block(me ^ 3, True), half_block(me ^ 3, False),
        half_block(me ^ 1, False), half_block(me ^ 2, True),
    ]


def panel_copies(me, j, pieces, panel, sems):
    copies = []
    for n, (piece, block) in enumerate(zip(pieces, piece_blocks(me)[NEW[j][0]:])):
        size = piece.shape[0]
        copies.append(
            pltpu.make_async_copy(piece, panel.at[pl.ds(pl.multiple_of(block * size, LANES), size)], sems.at[n])
        )
    return copies


def clear_panel(step, me, half, panel):
    for block in range(panel.shape[0] // half):
        @pl.when(arrival(jnp.int32(block), me) > step)
        def _():
            panel[block * half:(block + 1) * half, :] = jnp.zeros((half, panel.shape[1]), panel.dtype)


def row_tile(at, k, plan, map_ref, panel):
    return spread_tile(panel, map_ref, plan[at.row_begins + k], plan[at.row_base] + k * TILE)


def build_rows(at, first, last, plan, map_ref, panel, tiles, spread, sems):
    def written(k):
        return pltpu.make_async_copy(
            tiles.at[k], spread.at[pl.ds(pl.multiple_of(k * TILE, TILE), TILE)], sems.at[0]
        )

    def chosen(k):
        phase = plan[at.row_phases + k]
        return (phase >= first) & (phase <= last)

    @pl.loop(0, at.row_tiles)
    def _(k):
        @pl.when(chosen(k))
        def _():
            tiles[k] = row_tile(at, k, plan, map_ref, panel)
            written(k).start()

    @pl.loop(0, at.row_tiles)
    def _(k):
        pl.when(chosen(k))(lambda: written(k).wait())


def fetched(at, j, plan, front, fronts, sems, i):
    s = plan[at.lists + j * at.strips + i]
    slot = lax.rem(i, SLOTS)
    return pltpu.make_async_copy(
        front.at[:, pl.ds(pl.multiple_of(s * STRIP, STRIP), STRIP)], fronts.at[slot], sems.at[slot]
    )


def strips_begin(at, j, plan, front, fronts, sems, i):
    @pl.when(i < plan[at.counts + j])
    def _():
        fetched(at, j, plan, front, fronts, sems, jnp.int32(i)).start()


def begin(at, j, plan, front, fronts, sems, pieces, panel, own_sems, arriving):
    copies = panel_copies(plan[at.me], j, pieces, panel, own_sems)
    for copy in copies:
        copy.start()
    strips_begin(at, j, plan, front, fronts, sems, 0)
    for copy in arriving:
        copy.start()
    for i in range(1, SLOTS - 1):
        strips_begin(at, j, plan, front, fronts, sems, i)
    if j < 2:
        clear_panel(j, plan[at.me], pieces[0].shape[0] // 2, panel)
    for copy in copies:
        copy.wait()


def strips_loop(at, j, plan, front, fronts, sems, map_ref, panel, strips, total):
    count = plan[at.counts + j]
    listed = at.lists + j * at.strips

    @pl.when(count > 0)
    def _():
        strip_tile(at, plan[listed], plan, map_ref, panel, strips.at[0])

    @pl.loop(0, count)
    def _(i):
        @pl.when(i + SLOTS - 1 < count)
        def _():
            fetched(at, j, plan, front, fronts, sems, i + SLOTS - 1).start()

        now = lax.rem(i, 2)
        following = plan[listed + jnp.minimum(i + 1, count - 1)]
        fetched(at, j, plan, front, fronts, sems, i).wait()
        total[...] += jnp.dot(fronts[lax.rem(i, SLOTS)], strips[now], preferred_element_type=jnp.float32)
        strip_tile(at, following, plan, map_ref, panel, strips.at[1 - now])


def first_kernel(at, plan, front, map_ref, own, out, total, panel, fronts, strips, sems, own_sems):
    begin(at, 0, plan, front, fronts, sems, [own], panel, own_sems, [])
    total[...] = jnp.zeros_like(total)
    strips_loop(at, 0, plan, front, fronts, sems, map_ref, panel, strips, total)
    leaving = pltpu.make_async_copy(total, out, own_sems.at[0])
    leaving.start()
    leaving.wait()


def next_kernel(at, j, n_pieces, *refs):
    plan, front, map_ref = refs[:3]
    n_carried = 1 if j == 1 else 3
    start = refs[3]
    pieces = refs[3 + n_carried:3 + n_carried + n_pieces]
    outs = refs[3 + n_carried + n_pieces:-5]
    total, panel, spread = outs[:3]
    tiles, fronts, strips, sems, own_sems = refs[-5:]
    arriving = [pltpu.make_async_copy(start, total, own_sems.at[n_pieces])] if j == 1 else []
    begin(at, j, plan, front, fronts, sems, pieces, panel, own_sems, arriving)
    for copy in arriving:
        copy.wait()
    strips_loop(at, j, plan, front, fronts, sems, map_ref, panel, strips, total)
    if j == LAST:
        x_out, y_out, written = outs[3:]
        me = plan[at.me]
        coded = x_out.shape[0] // 2
        copy = pltpu.make_async_copy(total, written, own_sems.at[1])
        copy.start()
    build_rows(at, 0 if j == 1 else j, j, plan, map_ref, panel, tiles, spread, own_sems)
    if j == LAST:
        quantized(part_of(total, me ^ 3, 0), x_out.at[:coded])
        quantized(part_of(total, me ^ 1, 0), x_out.at[coded:])
        quantized(part_of(total, me ^ 3, 1), y_out.at[:coded])
        quantized(part_of(total, me ^ 2, 1), y_out.at[coded:])
        copy.wait()


def strips_call(kernel, at, plan, front, map3, others, carried, out_specs, out_shape, scratch, expected, name):
    rows = front.shape[0]
    width = out_shape[0].shape[1]
    vmem = pl.BlockSpec(memory_space=pltpu.VMEM)
    smem = pl.BlockSpec(memory_space=pltpu.SMEM)
    hbm = pl.BlockSpec(memory_space=pltpu.HBM)
    return pl.pallas_call(
        functools.partial(kernel, at),
        in_specs=[smem, hbm, vmem] + [vmem, vmem, hbm][:len(carried)] + [hbm] * len(others),
        out_specs=out_specs,
        scratch_shapes=scratch + [
            pltpu.VMEM((SLOTS, rows, STRIP), jnp.bfloat16),
            pltpu.VMEM((2, STRIP, width), jnp.bfloat16),
            pltpu.SemaphoreType.DMA((SLOTS,)),
            pltpu.SemaphoreType.DMA((len(others) + 2,)),
        ],
        out_shape=out_shape,
        input_output_aliases={3 + n: n for n in range(len(carried))},
        compiler_params=pltpu.CompilerParams(vmem_limit_bytes=LIMIT),
        cost_estimate=pl.CostEstimate(
            flops=8 * rows * STRIP * width * expected, bytes_accessed=8 * rows * STRIP * expected, transcendentals=0
        ) if expected else SMALL,
        name=name,
    )(plan, front, map3, *carried, *others)


def first_strips(at, plan, front, map3, own):
    rows, width = front.shape[0], own.shape[1]
    return strips_call(
        first_kernel, at, plan, front, map3, [own], [], [pl.BlockSpec(memory_space=pltpu.HBM)],
        [pltpu.HBM((rows, width), jnp.float32)],
        [pltpu.VMEM((rows, width), jnp.float32), pltpu.VMEM((map3.shape[0] * LANES, width), own.dtype)],
        FIRST, "strips_0",
    )[0]


def next_strips(at, j, plan, front, map3, pieces, carried):
    rows, width = front.shape[0], pieces[0].shape[1]
    vmem = pl.BlockSpec(memory_space=pltpu.VMEM)
    hbm = pl.BlockSpec(memory_space=pltpu.HBM)
    specs = [vmem, vmem, hbm]
    shapes = [
        pltpu.VMEM((rows, width), jnp.float32),
        pltpu.VMEM((map3.shape[0] * LANES, width), jnp.bfloat16),
        pltpu.HBM((rows, width), jnp.bfloat16),
    ]
    if j == LAST:
        payload = jax.ShapeDtypeStruct((2 * coded_rows(rows // 8), width), jnp.int16)
        specs += [vmem, vmem, hbm]
        shapes += [payload, payload, pltpu.HBM((rows, width), jnp.float32)]
    others, carried = (carried + pieces, []) if j == 1 else (pieces, carried)
    return strips_call(
        lambda at, *refs: next_kernel(at, j, len(pieces), *refs), at, plan, front, map3, others, carried, specs, shapes,
        [pltpu.VMEM((at.row_tiles, TILE, width), jnp.bfloat16)], 0 if j == LAST else at.strips, f"strips_{j}",
    )


def quantized(values, out_ref):
    rows, width = values.shape[0], values.shape[1]
    codes = []
    for g in range(rows // GROUP):
        part = values[g * GROUP:(g + 1) * GROUP, :]
        most = jnp.max(jnp.abs(part), axis=0, keepdims=True)
        code = jnp.clip(jnp.ceil(jnp.log2(jnp.maximum(most, 1e-30)) * STEPS) + 1.0, -32000.0, 32000.0)
        inverse = TOP / jnp.exp2(code * (1.0 / STEPS))
        whole = ((part * inverse + ROUND) - ROUND).astype(jnp.int32)
        out_ref[g * GROUP:(g + 1) * GROUP, :] = whole.astype(jnp.int16)
        codes.append(code)
    codes.append(jnp.zeros((out_ref.shape[0] - rows - len(codes), width), jnp.float32))
    tail = jnp.concatenate(codes, axis=0).astype(jnp.int32)
    out_ref[rows:, :] = tail.astype(jnp.int16)


def coded_rows(rows):
    return rows + (rows // GROUP + 15) // 16 * 16


def decoded(ref, rows):
    codes = ref[rows:, :].astype(jnp.int32).astype(jnp.float32)
    scales = jnp.exp2(codes * (1.0 / STEPS)) * (1.0 / TOP)
    parts = []
    for g in range(rows // GROUP):
        part = ref[g * GROUP:(g + 1) * GROUP, :].astype(jnp.int32).astype(jnp.float32)
        parts.append(part * scales[g:g + 1, :])
    return jnp.concatenate(parts, axis=0)


def part_of(total, which, part):
    half = total.shape[0] // 8
    return total[pl.ds(pl.multiple_of((which * 2 + part) * half, half), half), :]


def diag_kernel(at, plan, total, spread, *refs):
    outs, (sums, values, lefts, sems) = refs[:-4], refs[-4:]
    groups, rows = values.shape[:2]

    def blocks(group):
        place = pl.ds(pl.multiple_of(group * rows, rows), rows)
        return [
            pltpu.make_async_copy(total.at[place], values.at[group], sems.at[0, group]),
            pltpu.make_async_copy(spread.at[place], lefts.at[group], sems.at[1, group]),
        ]

    for group in range(groups):
        for copy in blocks(group):
            copy.start()
    sums[...] = jnp.zeros_like(sums)

    @pl.loop(0, groups)
    def _(group):
        for copy in blocks(group):
            copy.wait()
        high = values[group].astype(jnp.bfloat16)
        low = (values[group] - high.astype(jnp.float32)).astype(jnp.bfloat16)
        sums[...] += lax.dot_general(
            lefts[group], jnp.concatenate([high, low], axis=1), (((0,), (0,)), ((), ())),
            preferred_element_type=jnp.float32,
        )

    share, width = outs[0].shape
    for by, out in enumerate(outs):
        place = pl.ds(pl.multiple_of(lax.rem(plan[at.row] + by, len(outs)) * share, share), share)
        out[...] = sums[place, :width] + sums[place, width:]


def diag_product(at, plan, spread, total, shares):
    rows, width = total.shape
    chunk = GROUP_TILES * TILE
    vmem = pl.BlockSpec(memory_space=pltpu.VMEM)
    hbm = pl.BlockSpec(memory_space=pltpu.HBM)
    return pl.pallas_call(
        functools.partial(diag_kernel, at),
        in_specs=[pl.BlockSpec(memory_space=pltpu.SMEM), hbm, hbm],
        out_specs=[vmem] * shares,
        out_shape=[jax.ShapeDtypeStruct((width // shares, width), jnp.float32)] * shares,
        scratch_shapes=[
            pltpu.VMEM((width, 2 * width), jnp.float32),
            pltpu.VMEM((rows // chunk, chunk, width), jnp.float32),
            pltpu.VMEM((rows // chunk, chunk, width), jnp.bfloat16),
            pltpu.SemaphoreType.DMA((2, rows // chunk)),
        ],
        compiler_params=pltpu.CompilerParams(vmem_limit_bytes=LIMIT),
        cost_estimate=SMALL,
        name="diag_product",
    )(plan, total, spread)


def second_kernel(plan, low_ref, high_ref, x_in, y_in, low_out, high_out):
    rows = low_ref.shape[0]
    quantized(low_ref[...] + decoded(x_in, rows), low_out)
    quantized(high_ref[...] + decoded(y_in, rows), high_out)


def second_hop(at, plan, total, x_in, y_in):
    half, width = total.shape[0] // 8, total.shape[1]
    coded = x_in.shape[0] // 2
    payload = pl.BlockSpec((coded, width), lambda i, plan: (0, 0))
    return pl.pallas_call(
        second_kernel,
        grid_spec=pltpu.PrefetchScalarGridSpec(
            num_scalar_prefetch=1,
            grid=(1,),
            in_specs=[
                pl.BlockSpec((half, width), lambda i, plan: ((plan[at.me] ^ 2) * 2, 0)),
                pl.BlockSpec((half, width), lambda i, plan: ((plan[at.me] ^ 1) * 2 + 1, 0)),
                payload,
                payload,
            ],
            out_specs=[payload, payload],
        ),
        out_shape=[jax.ShapeDtypeStruct((coded, width), jnp.int16)] * 2,
        compiler_params=pltpu.CompilerParams(vmem_limit_bytes=LIMIT),
        cost_estimate=SMALL,
        name="second_hop",
    )(plan, total, total, x_in, y_in)


def terms_kernel(n, *refs):
    refs[-1][...] = sum((ref[...] for ref in refs[1:n]), refs[0][...])


def added(terms, after):
    vmem = pl.BlockSpec(memory_space=pltpu.VMEM)
    return pl.pallas_call(
        functools.partial(terms_kernel, len(terms)),
        in_specs=[vmem] * len(terms) + [pl.BlockSpec(memory_space=pl.ANY)] * len(after),
        out_specs=vmem,
        out_shape=jax.ShapeDtypeStruct(terms[0].shape, terms[0].dtype),
        compiler_params=pltpu.CompilerParams(vmem_limit_bytes=LIMIT),
        cost_estimate=SMALL,
        name="added",
    )(*terms, *after)


def gate_kernel(n, *refs):
    sems = refs[-1]
    copies = [
        pltpu.make_async_copy(source, out, sems.at[i]) for i, (source, out) in enumerate(zip(refs[:n], refs[-1 - n:-1]))
    ]
    for copy in copies:
        copy.start()
    for copy in copies:
        copy.wait()


def gated(values, after=()):
    return pl.pallas_call(
        functools.partial(gate_kernel, len(values)),
        in_specs=[pl.BlockSpec(memory_space=pl.ANY)] * (len(values) + len(after)),
        out_specs=[pl.BlockSpec(memory_space=pltpu.VMEM)] * len(values),
        out_shape=[pltpu.VMEM(value.shape, value.dtype) for value in values],
        scratch_shapes=[pltpu.SemaphoreType.DMA((len(values),))],
        compiler_params=pltpu.CompilerParams(vmem_limit_bytes=LIMIT),
        cost_estimate=SMALL,
        name="gated",
    )(*values, *after)


def last_kernel(at, plan, low_ref, high_ref, x_in, y_in, low_in, high_in, map_ref, out_ref):
    me = plan[at.me]
    rows = low_ref.shape[0]
    tiles = rows // TILE
    sums = [
        low_ref[...] + decoded(x_in, rows) + decoded(low_in, rows),
        high_ref[...] + decoded(y_in, rows) + decoded(high_in, rows),
    ]
    for part, value in enumerate(sums):
        for j in range(tiles):
            n = part * tiles + j
            k = me * 2 * tiles + n
            hits = window_hits(map_ref, plan[at.row_begins + k], plan[at.row_base] + k * TILE)
            marked = jnp.max(jnp.where(hits, 1.0, 0.0), axis=1, keepdims=True)
            tile = value[j * TILE:(j + 1) * TILE, :]
            out_ref[n * TILE:(n + 1) * TILE, :] = jnp.where(marked > 0.5, -tile, 0.0)


def last_sum(at, plan, total, x_in, y_in, low_in, high_in, map3):
    half, width = total.shape[0] // 8, total.shape[1]
    first = pl.BlockSpec(low_in.shape, lambda i, plan: (0, 0))
    second = pl.BlockSpec(low_in.shape, lambda i, plan: (1, 0))
    return pl.pallas_call(
        functools.partial(last_kernel, at),
        grid_spec=pltpu.PrefetchScalarGridSpec(
            num_scalar_prefetch=1,
            grid=(1,),
            in_specs=[
                pl.BlockSpec((half, width), lambda i, plan: (plan[at.me] * 2, 0)),
                pl.BlockSpec((half, width), lambda i, plan: (plan[at.me] * 2 + 1, 0)),
                second, second, first, first,
                pl.BlockSpec(map3.shape, lambda i, plan: (0, 0, 0)),
            ],
            out_specs=pl.BlockSpec((2 * half, width), lambda i, plan: (0, 0)),
        ),
        out_shape=pltpu.HBM((2 * half, width), jnp.float32),
        compiler_params=pltpu.CompilerParams(vmem_limit_bytes=LIMIT),
        cost_estimate=SMALL,
        name="last_sum",
    )(plan, total, total, x_in, y_in, low_in, high_in, map3)


def together_kernel(at, plan, start, *refs):
    shares, out = refs[:-2], refs[-1]
    for by, share in enumerate(shares):
        size = share.shape[0]
        place = pl.ds(pl.multiple_of(lax.rem(plan[at.row] - by + len(shares), len(shares)) * size, size), size)
        out[place, :] = start[place, :] + share[...]


def together(at, plan, start, shares, after):
    vmem = pl.BlockSpec(memory_space=pltpu.VMEM)
    return pl.pallas_call(
        functools.partial(together_kernel, at),
        in_specs=[pl.BlockSpec(memory_space=pltpu.SMEM), vmem] + [vmem] * len(shares)
        + [pl.BlockSpec(memory_space=pltpu.HBM)],
        out_specs=vmem,
        out_shape=jax.ShapeDtypeStruct(start.shape, start.dtype),
        compiler_params=pltpu.CompilerParams(vmem_limit_bytes=LIMIT),
        cost_estimate=SMALL,
        name="together",
    )(plan, start, *shares, after)


def four_columns(front, panel, row_map, diag_inverse):
    me = lax.axis_index("col")
    rows, cols = front.shape
    own = panel[0]
    half = own.shape[0] // 2
    places = row_map[0]
    map3 = places.reshape(-1, 1, LANES)
    total_rows = places.shape[0]
    at = Layout(rows, cols)

    def partner(value, bit):
        return lax.ppermute(value, "col", [(i, i ^ bit) for i in range(4)])

    def shifted(value, by):
        n = lax.axis_size("row")
        return lax.ppermute(value, "row", [(i, (i + by) % n) for i in range(n)])

    def in_hbm(value):
        return pltpu.with_memory_space_constraint(value, pltpu.HBM)

    own = in_hbm(own)
    near, far = halves(near_half(me).reshape(1), own)
    x_near = partner(near, 1)
    y_far = partner(far, 2)

    col_base = me * cols
    row_base = lax.axis_index("row") * rows
    marks = jnp.concatenate([
        col_base + TILE * jnp.arange(cols // TILE + 1, dtype=jnp.int32),
        row_base + TILE * jnp.arange(rows // TILE + 1, dtype=jnp.int32),
    ])
    before = jnp.sum(places[None, :] < marks[:, None], axis=1, dtype=jnp.int32)
    place = jnp.stack([me, col_base, row_base, lax.axis_index("row")]).astype(jnp.int32)
    plan = make_plan(at, half, total_rows, before, place)

    start = first_strips(at, plan, front, map3, own)
    x_on, y_on, far, near = gated([x_near, y_far, far, near])
    d_near = partner(x_on, 2)
    d_far = partner(y_on, 1)
    x_far = partner(far, 1)
    y_near = partner(near, 2)
    kept = next_strips(at, 1, plan, front, map3, [own, x_near, y_far], [in_hbm(start)])
    kept = next_strips(at, 2, plan, front, map3, [d_near, d_far], kept)
    *kept, to_x, to_y, total = next_strips(at, 3, plan, front, map3, [x_far, y_near], kept)
    total, spread = in_hbm(total), in_hbm(kept[2])
    from_x, from_y = partner(to_x, 1), partner(to_y, 2)
    n = lax.axis_size("row")
    terms = diag_product(at, plan, spread, total, n)
    terms = [terms[0]] + [shifted(terms[by], by) for by in range(1, n)]
    low, high = second_hop(at, plan, total, from_x, from_y)
    mine = sum(terms[1:], terms[0])
    terms = [mine] + [partner(mine, bit) for bit in (1, 2, 3)]
    low, high = gated([low, high], terms[1:])
    mine = sum(terms[1:], mine)
    low = partner(low, 2)
    high = partner(high, 1)
    offdiag = last_sum(at, plan, total, from_x, from_y, low, high, map3)
    diag = together(at, plan, diag_inverse[0], [mine] + [shifted(mine, by) for by in range(1, n)], in_hbm(offdiag))
    return offdiag[None], diag[None]


def spread_range(padded_rows, padded_places, places, lower, count):
    blk = math.gcd(count, 128)
    nblk = count // blk
    starts = lower + jnp.arange(nblk, dtype=jnp.int32) * blk
    first = jnp.searchsorted(places, starts)

    def window(begin):
        rows = lax.dynamic_slice_in_dim(padded_rows, begin, blk, 0)
        marks = lax.dynamic_slice_in_dim(padded_places, begin, blk, 0)
        return (rows, marks)

    rows, marks = jax.vmap(window)(first)
    target = starts[:, None] + jnp.arange(blk, dtype=jnp.int32)[None, :]
    onehot = marks[:, None, :] == target[:, :, None]
    table = onehot.astype(jnp.bfloat16)
    spread = jnp.einsum("njk,nkw->njw", table, rows, preferred_element_type=jnp.float32)
    hits = jnp.sum(onehot.astype(jnp.float32), axis=2)
    return (spread.astype(jnp.bfloat16).reshape(count, rows.shape[2]), hits.reshape(count))


def any_columns(front_inverse, panel, row_map, diag_inverse):
    row_index = lax.axis_index("row")
    col_index = lax.axis_index("col")
    ncol = lax.axis_size("col")
    front_rows, front_cols = front_inverse.shape
    share = front_rows // ncol
    width = panel.shape[2]
    col_lower = col_index * front_cols
    row_lower = row_index * front_rows
    share_lower = row_lower + col_index * share
    places_all = row_map[0]
    whole_panel = lax.all_gather(panel, "col", axis=1, tiled=True)[0]
    padded_rows = jnp.concatenate([whole_panel, jnp.zeros((128, width), jnp.bfloat16)], axis=0)
    total_front = front_rows * lax.axis_size("row")
    padded_places = jnp.concatenate([places_all, jnp.full((128,), total_front, jnp.int32)], axis=0)
    spread_cols, unused_hits = spread_range(
        padded_rows, padded_places, places_all, col_lower, front_cols
    )
    spread_rows, share_hits = spread_range(
        padded_rows, padded_places, places_all, share_lower, share
    )
    product = lax.psum_scatter(
        jnp.dot(front_inverse, spread_cols, preferred_element_type=jnp.float32),
        "col",
        scatter_dimension=0,
        tiled=True,
    )
    local_terms = jnp.dot(
        spread_rows.astype(jnp.float32).T, product, precision=lax.Precision.HIGHEST
    )
    diag_terms = lax.psum(local_terms, ("row", "col"))
    offdiag = jnp.where(share_hits[:, None] > 0.5, -product, jnp.zeros_like(product))
    diag = diag_inverse[0] + diag_terms
    return (offdiag[None], diag[None])


def solution(mesh):
    return jax.shard_map(
        four_columns if mesh.shape["col"] == 4 else any_columns,
        mesh=mesh,
        in_specs=(P("row", "col"), P("sib", "col", None), P("sib", None), P("sib", None, None)),
        out_specs=(P("sib", ("row", "col"), None), P("sib", None, None)),
        check_vma=False,
    )
```

```python
import functools

import jax
import jax.numpy as jnp
from jax import lax
from jax.experimental import pallas as pl
from jax.experimental.pallas import tpu as pltpu
from jax.sharding import PartitionSpec as P
import math

LANES = 128
TILE = 256
WINDOW = TILE + LANES
STRIP = 2 * TILE
SLOTS = 3
GROUP = 64
STEPS = 256.0
TOP = 32766.0
ROUND = 12582912.0
LIMIT = 38 * 1024 * 1024
FIRST = 3
KERNELS = 4
GROUP_TILES = 4
NEW = ((0, 1), (0, 3), (3, 5), (5, 7))
SMALL = pl.CostEstimate(flops=1000, bytes_accessed=1000, transcendentals=0)
LAST = 3


class Layout:
    def __init__(self, rows, cols):
        self.strips = cols // STRIP
        self.col_tiles = cols // TILE
        self.row_tiles = rows // TILE
        self.counts = 0
        self.lists = KERNELS
        self.col_begins = self.lists + KERNELS * self.strips
        self.row_begins = self.col_begins + self.col_tiles
        self.row_phases = self.row_begins + self.row_tiles
        self.me = self.row_phases + self.row_tiles
        self.col_base = self.me + 1
        self.row_base = self.me + 2
        self.row = self.me + 3
        self.size = self.me + 4


def near_half(shard):
    return 1 - lax.rem(shard, 2)


def arrival(block, me):
    shard = lax.div(block, 2)
    near = lax.rem(block, 2) == near_half(shard)
    away = shard ^ me
    beside = jnp.where(near == (away == 1), 1, 3)
    return jnp.where(away == 0, 0, jnp.where(away == 3, 2, beside))


def plan_kernel(at, half, total_rows, before, place, plan):
    me = place[0]

    def phase(first, last):
        start = arrival(lax.div(first, half), me)
        end = arrival(lax.div(last - 1, half), me)
        return jnp.maximum(start, end)

    def begin(first):
        return jnp.minimum(lax.div(first, LANES) * LANES, total_rows - WINDOW)

    for i in range(KERNELS * at.strips):
        plan[at.lists + i] = 0
    counts = [jnp.int32(0)] * KERNELS
    per = STRIP // TILE
    for s in range(at.strips):
        first, last = before[s * per], before[(s + 1) * per]
        when = phase(first, last)
        some = last > first
        taken = jnp.bool_(False)
        for j in range(KERNELS):
            fits = some & (when <= j) & ~taken
            if j == 0:
                fits = fits & (counts[j] < FIRST)

            @pl.when(fits)
            def _():
                plan[at.lists + j * at.strips + counts[j]] = s

            counts[j] = counts[j] + jnp.where(fits, 1, 0)
            taken = taken | fits
    for j in range(KERNELS):
        plan[at.counts + j] = counts[j]
    for k in range(at.col_tiles):
        plan[at.col_begins + k] = begin(before[k])
    base = at.col_tiles + 1
    for k in range(at.row_tiles):
        first, last = before[base + k], before[base + k + 1]
        plan[at.row_begins + k] = begin(first)
        plan[at.row_phases + k] = jnp.where(last > first, phase(first, last), 0)
    for i in range(4):
        plan[at.me + i] = place[i]


def make_plan(at, half, total_rows, before, place):
    smem = pl.BlockSpec(memory_space=pltpu.SMEM)
    return pl.pallas_call(
        functools.partial(plan_kernel, at, half, total_rows),
        in_specs=[smem, smem],
        out_specs=smem,
        out_shape=jax.ShapeDtypeStruct((at.size,), jnp.int32),
        compiler_params=pltpu.CompilerParams(vmem_limit_bytes=LIMIT),
        cost_estimate=SMALL,
        name="plan",
    )(before, place)


def halves_kernel(which, own, first, second, sems):
    half = first.shape[0]
    copies = [
        pltpu.make_async_copy(own.at[pl.ds(pl.multiple_of(part * half, LANES), half)], out, sems.at[n])
        for n, (part, out) in enumerate(((which[0], first), (1 - which[0], second)))
    ]
    for copy in copies:
        copy.start()
    for copy in copies:
        copy.wait()


def halves(which, own):
    piece = pltpu.VMEM((own.shape[0] // 2, own.shape[1]), own.dtype)
    vmem = pl.BlockSpec(memory_space=pltpu.VMEM)
    return pl.pallas_call(
        halves_kernel,
        in_specs=[pl.BlockSpec(memory_space=pltpu.SMEM), pl.BlockSpec(memory_space=pltpu.HBM)],
        out_specs=[vmem, vmem],
        out_shape=[piece, piece],
        scratch_shapes=[pltpu.SemaphoreType.DMA((2,))],
        compiler_params=pltpu.CompilerParams(vmem_limit_bytes=LIMIT),
        cost_estimate=SMALL,
        name="halves",
    )(which, own)


def window_hits(map_ref, begin, target):
    first = lax.div(begin, LANES)
    row = jnp.concatenate([map_ref[first + j] for j in range(WINDOW // LANES)], axis=1)
    wanted = lax.broadcasted_iota(jnp.int32, (TILE, WINDOW), 0) + target
    return wanted == row


def spread_tile(panel_ref, map_ref, begin, target):
    table = jnp.where(window_hits(map_ref, begin, target), 1.0, 0.0).astype(jnp.bfloat16)
    rows = panel_ref[pl.ds(pl.multiple_of(begin, LANES), WINDOW), :]
    return jnp.dot(table, rows, preferred_element_type=jnp.float32).astype(jnp.bfloat16)


def strip_tile(at, s, plan, map_ref, panel, strip):
    per = STRIP // TILE
    for t in range(per):
        k = s * per + t
        strip[t * TILE:(t + 1) * TILE, :] = spread_tile(
            panel, map_ref, plan[at.col_begins + k], plan[at.col_base] + k * TILE
        )


def half_block(shard, near):
    return shard * 2 + (near_half(shard) if near else 1 - near_half(shard))


def piece_blocks(me):
    return [
        me,
        half_block(me ^ 1, True), half_block(me ^ 2, False),
        half_block(me ^ 3, True), half_block(me ^ 3, False),
        half_block(me ^ 1, False), half_block(me ^ 2, True),
    ]


def panel_copies(me, j, pieces, panel, sems):
    copies = []
    for n, (piece, block) in enumerate(zip(pieces, piece_blocks(me)[NEW[j][0]:])):
        size = piece.shape[0]
        copies.append(
            pltpu.make_async_copy(piece, panel.at[pl.ds(pl.multiple_of(block * size, LANES), size)], sems.at[n])
        )
    return copies


def clear_panel(step, me, half, panel):
    for block in range(panel.shape[0] // half):
        @pl.when(arrival(jnp.int32(block), me) > step)
        def _():
            panel[block * half:(block + 1) * half, :] = jnp.zeros((half, panel.shape[1]), panel.dtype)


def row_tile(at, k, plan, map_ref, panel):
    return spread_tile(panel, map_ref, plan[at.row_begins + k], plan[at.row_base] + k * TILE)


def build_rows(at, first, last, plan, map_ref, panel, tiles, spread, sems):
    def written(k):
        return pltpu.make_async_copy(
            tiles.at[k], spread.at[pl.ds(pl.multiple_of(k * TILE, TILE), TILE)], sems.at[0]
        )

    def chosen(k):
        phase = plan[at.row_phases + k]
        return (phase >= first) & (phase <= last)

    def build(k):
        tiles[k] = row_tile(at, k, plan, map_ref, panel)
        written(k).start()

    @pl.loop(0, at.row_tiles // GROUP_TILES)
    def _(group):
        ks = [group * GROUP_TILES + t for t in range(GROUP_TILES)]
        every = chosen(ks[0])
        for k in ks[1:]:
            every = every & chosen(k)

        @pl.when(every)
        def _():
            for k in ks:
                build(k)

        @pl.when(~every)
        def _():
            for k in ks:
                pl.when(chosen(k))(functools.partial(build, k))

    @pl.loop(0, at.row_tiles)
    def _(k):
        pl.when(chosen(k))(lambda: written(k).wait())


def fetched(at, j, plan, front, fronts, sems, i):
    s = plan[at.lists + j * at.strips + i]
    slot = lax.rem(i, SLOTS)
    return pltpu.make_async_copy(
        front.at[:, pl.ds(pl.multiple_of(s * STRIP, STRIP), STRIP)], fronts.at[slot], sems.at[slot]
    )


def strips_begin(at, j, plan, front, fronts, sems, i):
    @pl.when(i < plan[at.counts + j])
    def _():
        fetched(at, j, plan, front, fronts, sems, jnp.int32(i)).start()


def begin(at, j, plan, front, fronts, sems, pieces, panel, own_sems, arriving):
    copies = panel_copies(plan[at.me], j, pieces, panel, own_sems)
    for copy in copies:
        copy.start()
    strips_begin(at, j, plan, front, fronts, sems, 0)
    for copy in arriving:
        copy.start()
    for i in range(1, SLOTS - 1):
        strips_begin(at, j, plan, front, fronts, sems, i)
    if j < 2:
        clear_panel(j, plan[at.me], pieces[0].shape[0] // 2, panel)
    for copy in copies:
        copy.wait()


def strips_loop(at, j, plan, front, fronts, sems, map_ref, panel, strips, total):
    count = plan[at.counts + j]
    listed = at.lists + j * at.strips

    @pl.when(count > 0)
    def _():
        strip_tile(at, plan[listed], plan, map_ref, panel, strips.at[0])

    @pl.loop(0, count)
    def _(i):
        @pl.when(i + SLOTS - 1 < count)
        def _():
            fetched(at, j, plan, front, fronts, sems, i + SLOTS - 1).start()

        now = lax.rem(i, 2)
        following = plan[listed + jnp.minimum(i + 1, count - 1)]
        fetched(at, j, plan, front, fronts, sems, i).wait()
        total[...] += jnp.dot(fronts[lax.rem(i, SLOTS)], strips[now], preferred_element_type=jnp.float32)
        strip_tile(at, following, plan, map_ref, panel, strips.at[1 - now])


def first_kernel(at, plan, front, map_ref, own, out, total, panel, fronts, strips, sems, own_sems):
    begin(at, 0, plan, front, fronts, sems, [own], panel, own_sems, [])
    total[...] = jnp.zeros_like(total)
    strips_loop(at, 0, plan, front, fronts, sems, map_ref, panel, strips, total)
    leaving = pltpu.make_async_copy(total, out, own_sems.at[0])
    leaving.start()
    leaving.wait()


def next_kernel(at, j, n_pieces, *refs):
    plan, front, map_ref = refs[:3]
    n_carried = 1 if j == 1 else 3
    start = refs[3]
    pieces = refs[3 + n_carried:3 + n_carried + n_pieces]
    outs = refs[3 + n_carried + n_pieces:-5]
    total, panel, spread = outs[:3]
    tiles, fronts, strips, sems, own_sems = refs[-5:]
    rows_args = (plan, map_ref, panel, tiles, spread, own_sems)
    if j < LAST:
        arriving = [pltpu.make_async_copy(start, total, own_sems.at[n_pieces])] if j == 1 else []
        begin(at, j, plan, front, fronts, sems, pieces, panel, own_sems, arriving)
        for copy in arriving:
            copy.wait()
        strips_loop(at, j, plan, front, fronts, sems, map_ref, panel, strips, total)
        build_rows(at, 0 if j == 1 else j, j, *rows_args)
        return

    x_out, y_out, written = outs[3:]
    me = plan[at.me]
    copies = panel_copies(me, j, pieces, panel, own_sems)
    leaving = pltpu.make_async_copy(total, written, own_sems.at[n_pieces])

    def send():
        coded = x_out.shape[0] // 2
        leaving.start()
        quantized(part_of(total, me ^ 3, 0), x_out.at[:coded])
        quantized(part_of(total, me ^ 1, 0), x_out.at[coded:])
        quantized(part_of(total, me ^ 3, 1), y_out.at[:coded])
        quantized(part_of(total, me ^ 2, 1), y_out.at[coded:])

    for copy in copies:
        copy.start()
    pl.when(plan[at.counts + j] == 0)(send)
    for copy in copies:
        copy.wait()

    @pl.when(plan[at.counts + j] > 0)
    def _():
        for i in range(SLOTS - 1):
            strips_begin(at, j, plan, front, fronts, sems, i)
        strips_loop(at, j, plan, front, fronts, sems, map_ref, panel, strips, total)
        send()

    build_rows(at, j, j, *rows_args)
    leaving.wait()


def strips_call(kernel, at, plan, front, map3, others, carried, out_specs, out_shape, scratch, expected, name):
    rows = front.shape[0]
    width = out_shape[0].shape[1]
    vmem = pl.BlockSpec(memory_space=pltpu.VMEM)
    smem = pl.BlockSpec(memory_space=pltpu.SMEM)
    hbm = pl.BlockSpec(memory_space=pltpu.HBM)
    return pl.pallas_call(
        functools.partial(kernel, at),
        in_specs=[smem, hbm, vmem] + [vmem, vmem, hbm][:len(carried)] + [hbm] * len(others),
        out_specs=out_specs,
        scratch_shapes=scratch + [
            pltpu.VMEM((SLOTS, rows, STRIP), jnp.bfloat16),
            pltpu.VMEM((2, STRIP, width), jnp.bfloat16),
            pltpu.SemaphoreType.DMA((SLOTS,)),
            pltpu.SemaphoreType.DMA((len(others) + 2,)),
        ],
        out_shape=out_shape,
        input_output_aliases={3 + n: n for n in range(len(carried))},
        compiler_params=pltpu.CompilerParams(vmem_limit_bytes=LIMIT),
        cost_estimate=pl.CostEstimate(
            flops=8 * rows * STRIP * width * expected, bytes_accessed=8 * rows * STRIP * expected, transcendentals=0
        ) if expected else SMALL,
        name=name,
    )(plan, front, map3, *carried, *others)


def first_strips(at, plan, front, map3, own):
    rows, width = front.shape[0], own.shape[1]
    return strips_call(
        first_kernel, at, plan, front, map3, [own], [], [pl.BlockSpec(memory_space=pltpu.HBM)],
        [pltpu.HBM((rows, width), jnp.float32)],
        [pltpu.VMEM((rows, width), jnp.float32), pltpu.VMEM((map3.shape[0] * LANES, width), own.dtype)],
        FIRST, "strips_0",
    )[0]


def next_strips(at, j, plan, front, map3, pieces, carried):
    rows, width = front.shape[0], pieces[0].shape[1]
    vmem = pl.BlockSpec(memory_space=pltpu.VMEM)
    hbm = pl.BlockSpec(memory_space=pltpu.HBM)
    specs = [vmem, vmem, hbm]
    shapes = [
        pltpu.VMEM((rows, width), jnp.float32),
        pltpu.VMEM((map3.shape[0] * LANES, width), jnp.bfloat16),
        pltpu.HBM((rows, width), jnp.bfloat16),
    ]
    if j == LAST:
        payload = jax.ShapeDtypeStruct((2 * coded_rows(rows // 8), width), jnp.int16)
        specs += [vmem, vmem, hbm]
        shapes += [payload, payload, pltpu.HBM((rows, width), jnp.float32)]
    others, carried = (carried + pieces, []) if j == 1 else (pieces, carried)
    return strips_call(
        lambda at, *refs: next_kernel(at, j, len(pieces), *refs), at, plan, front, map3, others, carried, specs, shapes,
        [pltpu.VMEM((at.row_tiles, TILE, width), jnp.bfloat16)], 0 if j == LAST else at.strips, f"strips_{j}",
    )


def quantized(values, out_ref):
    rows, width = values.shape[0], values.shape[1]
    codes = []
    for g in range(rows // GROUP):
        part = values[g * GROUP:(g + 1) * GROUP, :]
        most = jnp.max(jnp.abs(part), axis=0, keepdims=True)
        code = jnp.clip(jnp.ceil(jnp.log2(jnp.maximum(most, 1e-30)) * STEPS) + 1.0, -32000.0, 32000.0)
        inverse = TOP / jnp.exp2(code * (1.0 / STEPS))
        whole = ((part * inverse + ROUND) - ROUND).astype(jnp.int32)
        out_ref[g * GROUP:(g + 1) * GROUP, :] = whole.astype(jnp.int16)
        codes.append(code)
    codes.append(jnp.zeros((out_ref.shape[0] - rows - len(codes), width), jnp.float32))
    tail = jnp.concatenate(codes, axis=0).astype(jnp.int32)
    out_ref[rows:, :] = tail.astype(jnp.int16)


def coded_rows(rows):
    return rows + (rows // GROUP + 15) // 16 * 16


def decoded(ref, rows):
    codes = ref[rows:, :].astype(jnp.int32).astype(jnp.float32)
    scales = jnp.exp2(codes * (1.0 / STEPS)) * (1.0 / TOP)
    parts = []
    for g in range(rows // GROUP):
        part = ref[g * GROUP:(g + 1) * GROUP, :].astype(jnp.int32).astype(jnp.float32)
        parts.append(part * scales[g:g + 1, :])
    return jnp.concatenate(parts, axis=0)


def part_of(total, which, part):
    half = total.shape[0] // 8
    return total[pl.ds(pl.multiple_of((which * 2 + part) * half, half), half), :]


def diag_kernel(at, plan, total, spread, *refs):
    outs, (sums, values, lefts, sems) = refs[:-4], refs[-4:]
    groups, rows = values.shape[:2]

    def blocks(group):
        place = pl.ds(pl.multiple_of(group * rows, rows), rows)
        return [
            pltpu.make_async_copy(total.at[place], values.at[group], sems.at[0, group]),
            pltpu.make_async_copy(spread.at[place], lefts.at[group], sems.at[1, group]),
        ]

    for group in range(groups):
        for copy in blocks(group):
            copy.start()
    sums[...] = jnp.zeros_like(sums)

    @pl.loop(0, groups)
    def _(group):
        for copy in blocks(group):
            copy.wait()
        high = values[group].astype(jnp.bfloat16)
        low = (values[group] - high.astype(jnp.float32)).astype(jnp.bfloat16)
        sums[...] += lax.dot_general(
            lefts[group], jnp.concatenate([high, low], axis=1), (((0,), (0,)), ((), ())),
            preferred_element_type=jnp.float32,
        )

    share, width = outs[0].shape
    for by, out in enumerate(outs):
        place = pl.ds(pl.multiple_of(lax.rem(plan[at.row] + by, len(outs)) * share, share), share)
        out[...] = sums[place, :width] + sums[place, width:]


def diag_product(at, plan, spread, total, shares):
    rows, width = total.shape
    chunk = GROUP_TILES * TILE
    vmem = pl.BlockSpec(memory_space=pltpu.VMEM)
    hbm = pl.BlockSpec(memory_space=pltpu.HBM)
    return pl.pallas_call(
        functools.partial(diag_kernel, at),
        in_specs=[pl.BlockSpec(memory_space=pltpu.SMEM), hbm, hbm],
        out_specs=[vmem] * shares,
        out_shape=[jax.ShapeDtypeStruct((width // shares, width), jnp.float32)] * shares,
        scratch_shapes=[
            pltpu.VMEM((width, 2 * width), jnp.float32),
            pltpu.VMEM((rows // chunk, chunk, width), jnp.float32),
            pltpu.VMEM((rows // chunk, chunk, width), jnp.bfloat16),
            pltpu.SemaphoreType.DMA((2, rows // chunk)),
        ],
        compiler_params=pltpu.CompilerParams(vmem_limit_bytes=LIMIT),
        cost_estimate=SMALL,
        name="diag_product",
    )(plan, total, spread)


def own_block(total, which, part, block, sem):
    half = block.shape[0]
    return pltpu.make_async_copy(
        total.at[pl.ds(pl.multiple_of((which * 2 + part) * half, half), half)], block, sem
    )


def second_kernel(at, plan, total, x_in, y_in, low_out, high_out, low, high, sems):
    me = plan[at.me]
    rows, coded = low.shape[0], low_out.shape[0]
    copies = [own_block(total, me ^ 2, 0, low, sems.at[0]), own_block(total, me ^ 1, 1, high, sems.at[1])]
    for copy in copies:
        copy.start()
    copies[0].wait()
    quantized(low[...] + decoded(x_in.at[:coded], rows), low_out)
    copies[1].wait()
    quantized(high[...] + decoded(y_in.at[:coded], rows), high_out)


def second_hop(at, plan, total, x_in, y_in):
    half, width = total.shape[0] // 8, total.shape[1]
    vmem = pl.BlockSpec(memory_space=pltpu.VMEM)
    block = pltpu.VMEM((half, width), jnp.float32)
    return pl.pallas_call(
        functools.partial(second_kernel, at),
        in_specs=[pl.BlockSpec(memory_space=pltpu.SMEM), pl.BlockSpec(memory_space=pltpu.HBM), vmem, vmem],
        out_specs=[vmem, vmem],
        out_shape=[jax.ShapeDtypeStruct((x_in.shape[0] // 2, width), jnp.int16)] * 2,
        scratch_shapes=[block, block, pltpu.SemaphoreType.DMA((2,))],
        compiler_params=pltpu.CompilerParams(vmem_limit_bytes=LIMIT),
        cost_estimate=SMALL,
        name="second_hop",
    )(plan, total, x_in, y_in)


def gate_kernel(n, *refs):
    sems = refs[-1]
    copies = [
        pltpu.make_async_copy(source, out, sems.at[i]) for i, (source, out) in enumerate(zip(refs[:n], refs[-1 - n:-1]))
    ]
    for copy in copies:
        copy.start()
    for copy in copies:
        copy.wait()


def gated(values, after=()):
    return pl.pallas_call(
        functools.partial(gate_kernel, len(values)),
        in_specs=[pl.BlockSpec(memory_space=pl.ANY)] * (len(values) + len(after)),
        out_specs=[pl.BlockSpec(memory_space=pltpu.VMEM)] * len(values),
        out_shape=[pltpu.VMEM(value.shape, value.dtype) for value in values],
        scratch_shapes=[pltpu.SemaphoreType.DMA((len(values),))],
        compiler_params=pltpu.CompilerParams(vmem_limit_bytes=LIMIT),
        cost_estimate=SMALL,
        name="gated",
    )(*values, *after)


def last_kernel(at, plan, total, x_in, y_in, low_in, high_in, map_ref, out, blocks, sems):
    me = plan[at.me]
    parts, rows = blocks.shape[:2]
    coded = low_in.shape[0]
    tiles = rows // TILE
    copies = [own_block(total, me, part, blocks.at[part], sems.at[part]) for part in range(parts)]
    written = [
        pltpu.make_async_copy(blocks.at[part], out.at[pl.ds(part * rows, rows)], sems.at[parts + part])
        for part in range(parts)
    ]
    for copy in copies:
        copy.start()
    for part, (first, second) in enumerate(((x_in, low_in), (y_in, high_in))):
        more = decoded(first.at[coded:], rows) + decoded(second, rows)
        copies[part].wait()
        for j in range(tiles):
            k = (me * parts + part) * tiles + j
            hits = window_hits(map_ref, plan[at.row_begins + k], plan[at.row_base] + k * TILE)
            marked = jnp.max(jnp.where(hits, 1.0, 0.0), axis=1, keepdims=True)
            place = slice(j * TILE, (j + 1) * TILE)
            blocks[part, place, :] = jnp.where(marked > 0.5, -(blocks[part, place, :] + more[place, :]), 0.0)
        written[part].start()
    for copy in written:
        copy.wait()


def last_sum(at, plan, total, x_in, y_in, low_in, high_in, map3):
    half, width = total.shape[0] // 8, total.shape[1]
    vmem = pl.BlockSpec(memory_space=pltpu.VMEM)
    hbm = pl.BlockSpec(memory_space=pltpu.HBM)
    return pl.pallas_call(
        functools.partial(last_kernel, at),
        in_specs=[pl.BlockSpec(memory_space=pltpu.SMEM), hbm] + [vmem] * 5,
        out_specs=hbm,
        out_shape=pltpu.HBM((2 * half, width), jnp.float32),
        scratch_shapes=[pltpu.VMEM((2, half, width), jnp.float32), pltpu.SemaphoreType.DMA((4,))],
        compiler_params=pltpu.CompilerParams(vmem_limit_bytes=LIMIT),
        cost_estimate=SMALL,
        name="last_sum",
    )(plan, total, x_in, y_in, low_in, high_in, map3)


def together_kernel(at, plan, start, *refs):
    shares, out = refs[:-2], refs[-1]
    for by, share in enumerate(shares):
        size = share.shape[0]
        place = pl.ds(pl.multiple_of(lax.rem(plan[at.row] - by + len(shares), len(shares)) * size, size), size)
        out[place, :] = start[place, :] + share[...]


def together(at, plan, start, shares, after):
    vmem = pl.BlockSpec(memory_space=pltpu.VMEM)
    return pl.pallas_call(
        functools.partial(together_kernel, at),
        in_specs=[pl.BlockSpec(memory_space=pltpu.SMEM), vmem] + [vmem] * len(shares)
        + [pl.BlockSpec(memory_space=pltpu.HBM)],
        out_specs=vmem,
        out_shape=jax.ShapeDtypeStruct(start.shape, start.dtype),
        compiler_params=pltpu.CompilerParams(vmem_limit_bytes=LIMIT),
        cost_estimate=SMALL,
        name="together",
    )(plan, start, *shares, after)


def four_columns(front, panel, row_map, diag_inverse):
    me = lax.axis_index("col")
    rows, cols = front.shape
    own = panel[0]
    half = own.shape[0] // 2
    places = row_map[0]
    map3 = places.reshape(-1, 1, LANES)
    total_rows = places.shape[0]
    at = Layout(rows, cols)

    def partner(value, bit):
        return lax.ppermute(value, "col", [(i, i ^ bit) for i in range(4)])

    def shifted(value, by):
        n = lax.axis_size("row")
        return lax.ppermute(value, "row", [(i, (i + by) % n) for i in range(n)])

    def in_hbm(value):
        return pltpu.with_memory_space_constraint(value, pltpu.HBM)

    own = in_hbm(own)
    near, far = halves(near_half(me).reshape(1), own)
    x_near = partner(near, 1)
    y_far = partner(far, 2)

    col_base = me * cols
    row_base = lax.axis_index("row") * rows
    marks = jnp.concatenate([
        col_base + TILE * jnp.arange(cols // TILE + 1, dtype=jnp.int32),
        row_base + TILE * jnp.arange(rows // TILE + 1, dtype=jnp.int32),
    ])
    before = jnp.sum(places[None, :] < marks[:, None], axis=1, dtype=jnp.int32)
    place = jnp.stack([me, col_base, row_base, lax.axis_index("row")]).astype(jnp.int32)
    plan = make_plan(at, half, total_rows, before, place)

    start = first_strips(at, plan, front, map3, own)
    x_on, y_on, far, near = gated([x_near, y_far, far, near])
    d_near = partner(x_on, 2)
    d_far = partner(y_on, 1)
    x_far = partner(far, 1)
    y_near = partner(near, 2)
    kept = next_strips(at, 1, plan, front, map3, [own, x_near, y_far], [in_hbm(start)])
    kept = next_strips(at, 2, plan, front, map3, [d_near, d_far], kept)
    *kept, to_x, to_y, total = next_strips(at, 3, plan, front, map3, [x_far, y_near], kept)
    total, spread = in_hbm(total), in_hbm(kept[2])
    from_x, from_y = partner(to_x, 1), partner(to_y, 2)
    n = lax.axis_size("row")
    terms = diag_product(at, plan, spread, total, n)
    terms = [terms[0]] + [shifted(terms[by], by) for by in range(1, n)]
    low, high = second_hop(at, plan, total, from_x, from_y)
    mine = sum(terms[1:], terms[0])
    terms = [mine] + [partner(mine, bit) for bit in (1, 2, 3)]
    low, high = gated([low, high], terms[1:])
    mine = sum(terms[1:], mine)
    low = partner(low, 2)
    high = partner(high, 1)
    offdiag = last_sum(at, plan, total, from_x, from_y, low, high, map3)
    diag = together(at, plan, diag_inverse[0], [mine] + [shifted(mine, by) for by in range(1, n)], in_hbm(offdiag))
    return offdiag[None], diag[None]


def spread_range(padded_rows, padded_places, places, lower, count):
    blk = math.gcd(count, 128)
    nblk = count // blk
    starts = lower + jnp.arange(nblk, dtype=jnp.int32) * blk
    first = jnp.searchsorted(places, starts)

    def window(begin):
        rows = lax.dynamic_slice_in_dim(padded_rows, begin, blk, 0)
        marks = lax.dynamic_slice_in_dim(padded_places, begin, blk, 0)
        return (rows, marks)

    rows, marks = jax.vmap(window)(first)
    target = starts[:, None] + jnp.arange(blk, dtype=jnp.int32)[None, :]
    onehot = marks[:, None, :] == target[:, :, None]
    table = onehot.astype(jnp.bfloat16)
    spread = jnp.einsum("njk,nkw->njw", table, rows, preferred_element_type=jnp.float32)
    hits = jnp.sum(onehot.astype(jnp.float32), axis=2)
    return (spread.astype(jnp.bfloat16).reshape(count, rows.shape[2]), hits.reshape(count))


def any_columns(front_inverse, panel, row_map, diag_inverse):
    row_index = lax.axis_index("row")
    col_index = lax.axis_index("col")
    ncol = lax.axis_size("col")
    front_rows, front_cols = front_inverse.shape
    share = front_rows // ncol
    width = panel.shape[2]
    col_lower = col_index * front_cols
    row_lower = row_index * front_rows
    share_lower = row_lower + col_index * share
    places_all = row_map[0]
    whole_panel = lax.all_gather(panel, "col", axis=1, tiled=True)[0]
    padded_rows = jnp.concatenate([whole_panel, jnp.zeros((128, width), jnp.bfloat16)], axis=0)
    total_front = front_rows * lax.axis_size("row")
    padded_places = jnp.concatenate([places_all, jnp.full((128,), total_front, jnp.int32)], axis=0)
    spread_cols, unused_hits = spread_range(
        padded_rows, padded_places, places_all, col_lower, front_cols
    )
    spread_rows, share_hits = spread_range(
        padded_rows, padded_places, places_all, share_lower, share
    )
    product = lax.psum_scatter(
        jnp.dot(front_inverse, spread_cols, preferred_element_type=jnp.float32),
        "col",
        scatter_dimension=0,
        tiled=True,
    )
    local_terms = jnp.dot(
        spread_rows.astype(jnp.float32).T, product, precision=lax.Precision.HIGHEST
    )
    diag_terms = lax.psum(local_terms, ("row", "col"))
    offdiag = jnp.where(share_hits[:, None] > 0.5, -product, jnp.zeros_like(product))
    diag = diag_inverse[0] + diag_terms
    return (offdiag[None], diag[None])


def solution(mesh):
    return jax.shard_map(
        four_columns if mesh.shape["col"] == 4 else any_columns,
        mesh=mesh,
        in_specs=(P("row", "col"), P("sib", "col", None), P("sib", None), P("sib", None, None)),
        out_specs=(P("sib", ("row", "col"), None), P("sib", None, None)),
        check_vma=False,
    )
```
